512 devices in a mesh: dp: 2 (over core), space: 32 (over y, z_hi, x), filter: 8 (over z_lo).
Axes of the slice: x: 4, y: 4, z: 16 (z_hi: 2, z_lo: 8; z = z_hi * 8 + z_lo), core: 2. Of those that a mesh axis runs over, the one named last changes fastest.
Arguments:
- volumes: bfloat16 [2, 256, 32, 512], P('dp', 'filter', 'space'), may hold values from -6 to 6
- weight: bfloat16 [27, 256, 256], P(None, 'filter'), may hold values from -0.078125 to 0.078125
- bias: float32 [256], P('filter'), may hold values from -3 to 3
- cotangent: bfloat16 [2, 256, 32, 512], P('dp', 'filter', 'space'), may hold values from -6 to 6
Outputs:
- activations: bfloat16 [2, 256, 32, 512], P('dp', 'filter', 'space')
- grad_input: bfloat16 [2, 256, 32, 512], P('dp', 'filter', 'space')
- grad_weight: float32 [27, 256, 256], P(None, 'filter')
- grad_bias: float32 [256], P('filter')
The draws below stay inside these ranges and needn't reach their ends.
All inputs are finite; a program needn't handle non-finite values.
Results may differ from the reference program's by a relative error of at most 0.0075.
Values may be sent and summed in bfloat16 or wider, within the bound.
A program may use at most 64 MiB of HBM per device.

```python
import math
import jax
import jax.numpy as jnp
from jax import lax

C = 256
HEIGHT = 16
BREADTH = 32
TAPS = 27
VOLS = 2
XLEN = 32
FACE = 512


def steps_of(rng, dims, split, low, top_value):
    def one(dim, shards_of):
        steps = jax.random.uniform(jax.random.fold_in(jax.random.fold_in(rng, 6), dim), (shards_of,), jnp.float32, low / len(split), top_value / len(split))
        return jnp.repeat(jnp.exp(steps), dims[dim] // shards_of).reshape((-1,) + (1,) * (len(dims) - dim - 1))

    level = one(*split[0])
    for cut in split[1:]:
        level = level * one(*cut)
    return level


def noise(key, dims, scale, reach, shards=(), kind=jnp.bfloat16):
    gain = steps_of(key, dims, shards, -0.22, 0.18) if shards else 1.0
    array = jax.random.normal(key, dims, jnp.float32) * scale * gain
    return jnp.minimum(jnp.maximum(array, -reach), reach).astype(kind)


def setup_inputs(seed: int = 0) -> dict:
    splits = jax.random.split(jax.random.key(seed), 5)
    volumes = noise(splits[0], (VOLS, C, XLEN, FACE), 1.0, 6.0, ((0, 2), (1, 8), (2, 32)))
    weight = noise(splits[1], (TAPS, C, C), (27 * C) ** -0.5, 0.078125, ((1, 8),))
    bias = noise(splits[2], (C,), 0.5, 3.0, ((0, 8),), jnp.float32)
    cotangent = noise(splits[3], (VOLS, C, XLEN, FACE), 1.0, 6.0, ((0, 2), (1, 8), (2, 32)))
    return dict(volumes=volumes, weight=weight, bias=bias, cotangent=cotangent)


plane_steps = [(-1, -1), (-1, 0), (-1, 1), (0, -1), (0, 0), (0, 1), (1, -1), (1, 0), (1, 1)]

def shift_plane(block, step_row, step_col):
    face_len = HEIGHT * BREADTH
    margin = BREADTH + 1
    widths = [(0, 0)] * (block.ndim - 1) + [(margin, margin)]
    padded = jnp.pad(block, widths)
    offset = step_row * BREADTH + step_col
    moved = lax.slice_in_dim(padded, margin + offset, margin + offset + face_len, axis=block.ndim - 1)
    position = jnp.arange(face_len, dtype=jnp.int32)
    row_index = position // BREADTH + step_row
    col_index = position % BREADTH + step_col
    inside = (row_index >= 0) & (row_index < HEIGHT) & (col_index >= 0) & (col_index < BREADTH)
    return moved * inside.astype(block.dtype)

def depth_stack(shifted, planes, starts):
    pieces = [lax.slice_in_dim(shifted, begin, begin + planes, axis=1) for begin in starts]
    joined = jnp.concatenate(pieces, axis=0)
    return joined.reshape(joined.shape[0], planes * joined.shape[2])

def forward_terms(padded, weight):
    planes = padded.shape[1] - 2
    grouped = weight.reshape(3, 9, weight.shape[1], weight.shape[2]).astype(jnp.float32)
    total = jnp.zeros((weight.shape[1], planes * padded.shape[2]), jnp.float32)
    for index, (step_row, step_col) in enumerate(plane_steps):
        stacked = depth_stack(shift_plane(padded, step_row, step_col), planes, (0, 1, 2)).astype(jnp.float32)
        taps = jnp.transpose(grouped[:, index], (1, 0, 2)).reshape(weight.shape[1], 3 * weight.shape[2])
        total = total + jnp.dot(taps, stacked, preferred_element_type=jnp.float32)
    return total

def weight_terms(padded, grad):
    planes = padded.shape[1] - 2
    parts = []
    for step_row, step_col in plane_steps:
        stacked = depth_stack(shift_plane(padded, step_row, step_col), planes, (0, 1, 2)).astype(jnp.float32)
        term = lax.dot_general(grad.astype(jnp.float32), stacked, (((1,), (1,)), ((), ())), preferred_element_type=jnp.float32)
        parts.append(term.reshape(grad.shape[0], 3, padded.shape[0]))
    joined = jnp.transpose(jnp.stack(parts), (2, 0, 1, 3))
    return joined.reshape(27, grad.shape[0], padded.shape[0])

def input_terms(grad_pad, slab):
    planes = grad_pad.shape[1] - 2
    grouped = slab.reshape(3, 9, slab.shape[1], slab.shape[2]).astype(jnp.float32)
    total = jnp.zeros((slab.shape[2], planes * grad_pad.shape[2]), jnp.float32)
    for index, (step_row, step_col) in enumerate(plane_steps):
        stacked = depth_stack(shift_plane(grad_pad, -step_row, -step_col), planes, (2, 1, 0)).astype(jnp.float32)
        taps = grouped[:, index].reshape(3 * slab.shape[1], slab.shape[2])
        total = total + lax.dot_general(taps, stacked, (((0,), (0,)), ((), ())), preferred_element_type=jnp.float32)
    return total

def reference(volumes, weight, bias, cotangent):
    outputs = []
    grads_in = []
    weight_total = jnp.zeros((27, C, C), jnp.float32)
    bias_total = jnp.zeros((C,), jnp.float32)
    for volume in range(VOLS):
        padded = jnp.pad(volumes[volume], ((0, 0), (1, 1), (0, 0)))
        pre = forward_terms(padded, weight) + bias[:, None]
        sig = jax.nn.sigmoid(pre)
        outputs.append((pre * sig).astype(jnp.bfloat16).reshape(C, XLEN, FACE))
        upstream = cotangent[volume].reshape(C, XLEN * FACE).astype(jnp.float32)
        grad = (upstream * sig * (1.0 + pre * (1.0 - sig))).astype(jnp.bfloat16)
        weight_total = weight_total + weight_terms(padded, grad)
        bias_total = bias_total + lax.optimization_barrier(jnp.sum(grad.astype(jnp.float32), axis=1))
        grad_pad = jnp.pad(grad.reshape(C, XLEN, FACE), ((0, 0), (1, 1), (0, 0)))
        grads_in.append(input_terms(grad_pad, weight).astype(jnp.bfloat16).reshape(C, XLEN, FACE))
    scale = 1.0 / math.sqrt(VOLS * XLEN * FACE)
    return (jnp.stack(outputs), jnp.stack(grads_in), weight_total * scale, bias_total * scale)
```

```python
import functools
import math

import jax
import jax.numpy as jnp
from jax import lax
from jax.experimental import pallas as pl
from jax.experimental.pallas import tpu as pltpu
from jax.sharding import PartitionSpec as P

HEIGHT = 16
BREADTH = 32
FACE = HEIGHT * BREADTH
ROWS = 32
CHANNELS = 256
TAPS = 27
UNITS = 28
OWNERS = UNITS // 2
MESH = pl.DeviceIdType.MESH
F32 = jnp.float32
BF16 = jnp.bfloat16
SHIFTS = [(b, c) for b in (-1, 0, 1) for c in (-1, 0, 1)]


def masks():
    f = lax.broadcasted_iota(jnp.int32, (ROWS, FACE), 1)
    row, col = f // BREADTH, f % BREADTH
    row_ok = {b: (row + b >= 0) & (row + b < HEIGHT) for b in (-1, 1)}
    col_ok = {c: (col + c >= 0) & (col + c < BREADTH) for c in (-1, 1)}
    return row_ok, col_ok


def pull(x, amount, ok):
    return jnp.where(ok, pltpu.roll(x, (-amount) % FACE, 1), 0.0)


def pack(v):
    high = v.astype(BF16).astype(F32)
    low = v - high
    row = lax.broadcasted_iota(jnp.int32, (16, CHANNELS), 0)
    return jnp.where(row == 0, high, jnp.where(row == 1, low, 0.0)).astype(BF16)


def unpack(unit):
    u = unit.astype(F32)
    row = lax.broadcasted_iota(jnp.int32, u.shape, 0)
    return jnp.sum(jnp.where(row < 2, u, 0.0), axis=0, keepdims=True)


def kernel(
    scale,
    vol, w, bias, cot,
    act_o, gin_o, gw_o, gb_o,
    V, COT, QS, QR, Q0, ACT, GN, GS, Fp, S, R0, T1, R1, O, N, RG,
    z_send, z_recv, c_sem, q_send, q_recv, g_send, g_recv,
    d_sem, rs_send, rs_recv, ag_send, ag_recv, e_sem, n_send, n_recv,
):
    d = lax.axis_index("dp")
    s = lax.axis_index("space")
    f = lax.axis_index("filter")
    y = s // 8
    zh = (s // 4) % 2
    x = s % 4
    z = zh * 8 + f
    me = y * 4 + x

    def at_z(k):
        return (d, y * 8 + (k // 8) * 4 + x, k % 8)

    def at_xy(j):
        return (d, (j // 4) * 8 + zh * 4 + j % 4, f)

    def near(k):
        return (z + k + 16) % 16

    other = (1 - d, s, f)

    def copy(src, dst, send, recv, to):
        return pltpu.make_async_remote_copy(
            src_ref=src, dst_ref=dst, send_sem=send, recv_sem=recv,
            device_id=to, device_id_type=MESH,
        )

    barrier = pltpu.get_barrier_semaphore()
    for k in range(1, 16):
        pl.semaphore_signal(barrier, inc=1, device_id=at_z((z + k) % 16), device_id_type=MESH)
        pl.semaphore_signal(barrier, inc=1, device_id=at_xy((me + k) % 16), device_id_type=MESH)
    pl.semaphore_signal(barrier, inc=1, device_id=other, device_id_type=MESH)
    pl.semaphore_wait(barrier, 31)

    even = z % 2 == 0
    step2 = jnp.where(even, 2, -2)
    nears = [near(1), near(-1), (z + step2 + 16) % 16]
    fars = [near(4), near(-4), near(8)]
    V[z] = vol[...]
    COT[zh] = cot[...]
    sends = []

    def shard(slot, to, i):
        c = copy(V.at[slot], V.at[slot], z_send.at[i], z_recv.at[slot], at_z(to))
        c.start()
        sends.append(c)

    def shard_wait(slot):
        copy(V.at[slot], V.at[slot], z_send.at[0], z_recv.at[slot], at_z(nears[0])).wait_recv()

    for i, to in enumerate(fars + nears):
        shard(z, to, i)
    for j, slot in enumerate(fars):
        shard_wait(slot)
        for i, to in enumerate(nears):
            shard(slot, to, 6 + 3 * j + i)
    cot_copy = copy(COT.at[zh], COT.at[zh], c_sem.at[0], c_sem.at[1], at_z(near(8)))
    cot_copy.start()
    sources = [near(1), near(-1), (z - step2 + 16) % 16]
    for far in (0, 4, -4, 8):
        for source in sources:
            shard_wait((source + far + 16) % 16)

    row_ok, col_ok = masks()

    def contribution(p, a):
        plane = V[8 * p : 8 * p + 8].reshape(CHANNELS, FACE)
        taps = w[(a + 1) * 9 * ROWS : (a + 2) * 9 * ROWS, :]
        prod = jnp.dot(taps, plane, preferred_element_type=F32)
        total = None
        for c in (0, -1, 1):
            part = None
            for b in (0, -1, 1):
                i = 3 * (b + 1) + (c + 1)
                term = prod[i * ROWS : (i + 1) * ROWS]
                if b:
                    term = pull(term, BREADTH * b, row_ok[b])
                part = term if part is None else part + term
            if c:
                part = pull(part, c, col_ok[c])
            total = part if total is None else total + part
        return total

    def after(p):
        last = x == 3
        x2 = (x + 1) % 4
        y2 = (y + jnp.where(last, p, 0)) % 4
        return y2 * 4 + x2, jnp.where(last, 1 - p, p)

    def before(p):
        first = x == 0
        x2 = (x + 3) % 4
        y2 = (y + 4 - jnp.where(first, 1 - p, 0)) % 4
        return y2 * 4 + x2, jnp.where(first, 1 - p, p)

    q_copies = []
    for p in (0, 1):
        for side, a, where in ((0, -1, after), (1, 1, before)):
            QS[p, side] = contribution(p, a).astype(BF16)
            j, q = where(p)
            c = copy(QS.at[p, side], QR.at[q, side], q_send.at[p, side], q_recv.at[q, side], at_xy(j))
            c.start()
            q_copies.append(c)
    for p in (0, 1):
        Q0[p] = contribution(p, 0)
    eye = lax.broadcasted_iota(jnp.int32, (ROWS, ROWS), 0) == lax.broadcasted_iota(
        jnp.int32, (ROWS, ROWS), 1
    )
    column = jnp.sum(jnp.where(eye, bias[...], 0.0), axis=1, keepdims=True)
    first_plane = (y == 0) & (x == 0)
    last_plane = (y == 3) & (x == 3)
    cot_copy.wait_recv()
    g_copies = []
    bias_total = jnp.zeros((ROWS, 1), F32)
    for p in (0, 1):
        for side in (0, 1):
            copy(
                QS.at[p, side], QR.at[p, side], q_send.at[p, side], q_recv.at[p, side], other
            ).wait_recv()
        before_term = QR[p, 0].astype(F32)
        after_term = QR[p, 1].astype(F32)
        if p == 0:
            before_term = jnp.where(first_plane, 0.0, before_term)
        else:
            after_term = jnp.where(last_plane, 0.0, after_term)
        pre = Q0[p] + before_term + after_term + column
        sig = jax.nn.sigmoid(pre)
        grad = (COT[p].astype(F32) * sig * (1.0 + pre * (1.0 - sig))).astype(BF16)
        GN[p, 1] = grad
        for side, slot, where in ((0, 2, after), (1, 0, before)):
            j, q = where(p)
            c = copy(GN.at[p, 1], GN.at[q, slot], g_send.at[p, side], g_recv.at[q, side], at_xy(j))
            c.start()
            g_copies.append(c)
        ACT[p] = (pre * sig).astype(BF16)
        bias_total = bias_total + jnp.sum(grad.astype(F32), axis=1, keepdims=True)
    act_o[...] = ACT[zh]

    def shifted(p, a):
        grad = GN[p, a + 1].astype(F32)
        if p == 0 and a == 1:
            grad = jnp.where(first_plane, 0.0, grad)
        if p == 1 and a == -1:
            grad = jnp.where(last_plane, 0.0, grad)
        for c in (-1, 0, 1):
            moved = pull(grad, -c, col_ok[-c]) if c else grad
            for b in (-1, 0, 1):
                t = 9 * (a + 1) + 3 * (b + 1) + (c + 1)
                term = pull(moved, -BREADTH * b, row_ok[-b]) if b else moved
                GS[p, t * ROWS : (t + 1) * ROWS, :] = term.astype(BF16)

    def weight_grad(a):
        rows = slice((a + 1) * 9 * ROWS, (a + 2) * 9 * ROWS)
        total = None
        for p in (0, 1):
            plane = V[8 * p : 8 * p + 8].reshape(CHANNELS, FACE)
            term = lax.dot_general(
                GS[p, rows, :], plane, (((1,), (1,)), ((), ())), preferred_element_type=F32
            )
            total = term if total is None else total + term
        for i in range(9):
            t = 9 * (a + 1) + i
            for h in (0, 1):
                piece = total[i * ROWS + h * 16 : i * ROWS + (h + 1) * 16]
                Fp[h, t] = piece
                S[h, t] = piece.astype(BF16)

    for p in (0, 1):
        shifted(p, 0)
    weight_grad(0)
    eye = lax.broadcasted_iota(jnp.int32, (ROWS, CHANNELS), 0) == lax.broadcasted_iota(
        jnp.int32, (ROWS, CHANNELS), 1
    )
    bias_row = jnp.sum(jnp.where(eye, bias_total, 0.0), axis=0, keepdims=True)
    for h in (0, 1):
        Fp[h, TAPS] = jnp.broadcast_to(bias_row, (16, CHANNELS))
        S[h, TAPS] = pack(bias_row)
    for p in (0, 1):
        for side, slot in ((0, 2), (1, 0)):
            copy(
                GN.at[p, 1], GN.at[p, slot], g_send.at[p, side], g_recv.at[p, side], other
            ).wait_recv()
    for a in (-1, 1):
        for p in (0, 1):
            shifted(p, a)
        weight_grad(a)

    d_copy = copy(S.at[1 - d], R0, d_sem.at[0], d_sem.at[1], other)
    d_copy.start()

    part = lax.dot_general(
        w[...], GS[zh], (((0,), (0,)), ((), ())), preferred_element_type=F32
    )
    for i in range(8):
        N[i] = part[i * ROWS : (i + 1) * ROWS].astype(BF16)
    n_copies = []
    for k in range(1, 8):
        to = (f + k) % 8
        c = copy(N.at[to], RG.at[f], n_send.at[k], n_recv.at[f], (d, s, to))
        c.start()
        n_copies.append(c)

    d_copy.wait_recv()
    summed = Fp[d] + R0[...].astype(F32)
    T1[...] = summed.astype(BF16)
    T1[TAPS] = pack(Fp[d, TAPS, 0:1, :] + unpack(R0[TAPS]))

    def mine(ref, j):
        return ref.at[pl.ds(2 * j, 2)]

    def rs_copy(k):
        to = (me + k) % 16
        return to, copy(mine(T1, to), mine(R1, me), rs_send.at[k], rs_recv.at[me], at_xy(to))

    for k in range(1, 16):
        to, c = rs_copy(k)
        pl.when(to < OWNERS)(c.start)

    @pl.when(me < OWNERS)
    def _():
        R1[pl.ds(2 * me, 2)] = T1[pl.ds(2 * me, 2)]
        for k in range(1, 16):
            source = (me + k) % 16
            copy(
                mine(T1, me), mine(R1, source), rs_send.at[k], rs_recv.at[source], at_xy(source)
            ).wait_recv()
        total = R1[0:2].astype(F32)
        for i in range(1, 16):
            total = total + R1[2 * i : 2 * i + 2].astype(F32)
        O[d, pl.ds(2 * me, 2)] = total.astype(BF16)

        @pl.when(me == OWNERS - 1)
        def _():
            O[d, TAPS] = pack(jnp.sum(total[1, 0:2], axis=0, keepdims=True))

        for k in range(1, 16):
            to = (me + k) % 16
            copy(
                O.at[d, pl.ds(2 * me, 2)], O.at[d, pl.ds(2 * me, 2)],
                ag_send.at[k], ag_recv.at[me], at_xy(to),
            ).start()

    own = N[f].astype(F32)
    for k in range(1, 8):
        source = (f + k) % 8
        copy(N.at[source], RG.at[source], n_send.at[k], n_recv.at[source], (d, s, source)).wait_recv()
        own = own + RG[source].astype(F32)
    gin_o[...] = own.astype(BF16)

    for k in range(1, 16):
        source = (me + k) % 16

        @pl.when(source < OWNERS)
        def _():
            copy(
                O.at[d, pl.ds(2 * source, 2)], O.at[d, pl.ds(2 * source, 2)],
                ag_send.at[k], ag_recv.at[source], at_xy(source),
            ).wait_recv()

    e_copy = copy(O.at[d], O.at[d], e_sem.at[0], e_sem.at[1], other)
    e_copy.start()

    def finish(h):
        gw_o[:, pl.ds(pl.multiple_of(h * 16, 16), 16), :] = O[h, 0:TAPS].astype(F32) * scale

    finish(d)
    copy(O.at[1 - d], O.at[1 - d], e_sem.at[0], e_sem.at[1], other).wait_recv()
    finish(1 - d)
    gb_o[...] = unpack(O[0, TAPS])[:, :128] * scale

    for c in sends + q_copies + g_copies + n_copies + [cot_copy, d_copy, e_copy]:
        c.wait_send()
    for k in range(1, 16):
        to, c = rs_copy(k)
        pl.when(to < OWNERS)(c.wait_send)

    @pl.when(me < OWNERS)
    def _():
        for k in range(1, 16):
            to = (me + k) % 16
            copy(
                O.at[d, pl.ds(2 * me, 2)], O.at[d, pl.ds(2 * me, 2)],
                ag_send.at[k], ag_recv.at[me], at_xy(to),
            ).wait_send()


def per_device(scale, volumes, weight, bias, cotangent):
    vmem = pl.BlockSpec(memory_space=pltpu.VMEM)
    dma = pltpu.SemaphoreType.DMA
    act, gin, gw, gb = pl.pallas_call(
        functools.partial(kernel, scale),
        out_shape=[
            jax.ShapeDtypeStruct((ROWS, FACE), BF16),
            jax.ShapeDtypeStruct((ROWS, FACE), BF16),
            jax.ShapeDtypeStruct((TAPS, ROWS, CHANNELS), F32),
            jax.ShapeDtypeStruct((1, 128), F32),
        ],
        in_specs=[vmem] * 4,
        out_specs=[vmem] * 4,
        scratch_shapes=[
            pltpu.VMEM((16, ROWS, FACE), BF16),
            pltpu.VMEM((2, ROWS, FACE), BF16),
            pltpu.VMEM((2, 2, ROWS, FACE), BF16),
            pltpu.VMEM((2, 2, ROWS, FACE), BF16),
            pltpu.VMEM((2, ROWS, FACE), F32),
            pltpu.VMEM((2, ROWS, FACE), BF16),
            pltpu.VMEM((2, 3, ROWS, FACE), BF16),
            pltpu.VMEM((2, TAPS * ROWS, FACE), BF16),
            pltpu.VMEM((2, UNITS, 16, CHANNELS), F32),
            pltpu.VMEM((2, UNITS, 16, CHANNELS), BF16),
            pltpu.VMEM((UNITS, 16, CHANNELS), BF16),
            pltpu.VMEM((UNITS, 16, CHANNELS), BF16),
            pltpu.VMEM((32, 16, CHANNELS), BF16),
            pltpu.VMEM((2, UNITS, 16, CHANNELS), BF16),
            pltpu.VMEM((8, ROWS, FACE), BF16),
            pltpu.VMEM((8, ROWS, FACE), BF16),
            dma((15,)), dma((16,)), dma((2,)),
            dma((2, 2)), dma((2, 2)), dma((2, 2)), dma((2, 2)),
            dma((2,)), dma((16,)), dma((16,)), dma((16,)), dma((16,)), dma((2,)),
            dma((8,)), dma((8,)),
        ],
        compiler_params=pltpu.CompilerParams(
            collective_id=0, has_side_effects=True, vmem_limit_bytes=48 * 2**20
        ),
    )(
        volumes.reshape(ROWS, FACE),
        weight.reshape(TAPS * ROWS, CHANNELS),
        bias.reshape(1, ROWS),
        cotangent.reshape(ROWS, FACE),
    )
    shape = (1, ROWS, 1, FACE)
    return act.reshape(shape), gin.reshape(shape), gw, gb[0, :ROWS]


def solution(mesh):
    scale = 1.0 / math.sqrt(2 * 32 * FACE)
    return jax.shard_map(
        functools.partial(per_device, scale),
        mesh=mesh,
        in_specs=(
            P("dp", "filter", "space", None),
            P(None, "filter", None),
            P("filter"),
            P("dp", "filter", "space", None),
        ),
        out_specs=(
            P("dp", "filter", "space", None),
            P("dp", "filter", "space", None),
            P(None, "filter", None),
            P("filter"),
        ),
        check_vma=False,
    )
```

```python
import functools
import math

import jax
import jax.numpy as jnp
from jax import lax
from jax.experimental import pallas as pl
from jax.experimental.pallas import tpu as pltpu
from jax.sharding import PartitionSpec as P

HEIGHT = 16
BREADTH = 32
FACE = HEIGHT * BREADTH
ROWS = 32
CHANNELS = 256
TAPS = 27
UNITS = 28
OWNERS = UNITS // 2
MESH = pl.DeviceIdType.MESH
F32 = jnp.float32
BF16 = jnp.bfloat16
SHIFTS = [(b, c) for b in (-1, 0, 1) for c in (-1, 0, 1)]


def masks():
    f = lax.broadcasted_iota(jnp.int32, (ROWS, FACE), 1)
    row, col = f // BREADTH, f % BREADTH
    row_ok = {b: (row + b >= 0) & (row + b < HEIGHT) for b in (-1, 1)}
    col_ok = {c: (col + c >= 0) & (col + c < BREADTH) for c in (-1, 1)}
    return row_ok, col_ok


def pull(x, amount, ok):
    return jnp.where(ok, pltpu.roll(x, (-amount) % FACE, 1), 0.0)


def pack(v):
    high = v.astype(BF16).astype(F32)
    low = v - high
    row = lax.broadcasted_iota(jnp.int32, (16, CHANNELS), 0)
    return jnp.where(row == 0, high, jnp.where(row == 1, low, 0.0)).astype(BF16)


def unpack(unit):
    u = unit.astype(F32)
    row = lax.broadcasted_iota(jnp.int32, u.shape, 0)
    return jnp.sum(jnp.where(row < 2, u, 0.0), axis=0, keepdims=True)


def kernel(
    scale,
    vol, w, bias, cot,
    act_o, gin_o, gw_o, gb_o,
    V, COT, QS, QR, Q0, ACT, GN, GS, Fp, S, R0, T1, R1, O, N, RG,
    W, B, in_sem, z_send, z_recv, c_sem, q_send, q_recv, g_send, g_recv,
    d_sem, rs_send, rs_recv, ag_send, ag_recv, e_sem, n_send, n_recv,
):
    d = lax.axis_index("dp")
    s = lax.axis_index("space")
    f = lax.axis_index("filter")
    y = s // 8
    zh = (s // 4) % 2
    x = s % 4
    z = zh * 8 + f
    me = y * 4 + x

    def at_z(k):
        return (d, y * 8 + (k // 8) * 4 + x, k % 8)

    def at_xy(j):
        return (d, (j // 4) * 8 + zh * 4 + j % 4, f)

    def near(k):
        return (z + k + 16) % 16

    other = (1 - d, s, f)

    def copy(src, dst, send, recv, to):
        return pltpu.make_async_remote_copy(
            src_ref=src, dst_ref=dst, send_sem=send, recv_sem=recv,
            device_id=to, device_id_type=MESH,
        )

    barrier = pltpu.get_barrier_semaphore()
    for k in range(1, 16):
        pl.semaphore_signal(barrier, inc=1, device_id=at_z((z + k) % 16), device_id_type=MESH)
        pl.semaphore_signal(barrier, inc=1, device_id=at_xy((me + k) % 16), device_id_type=MESH)
    pl.semaphore_signal(barrier, inc=1, device_id=other, device_id_type=MESH)
    loads = [
        pltpu.make_async_copy(src, dst, in_sem.at[i])
        for i, (src, dst) in enumerate(
            ((vol, V.at[z]), (cot, COT.at[zh]), (w, W), (bias, B))
        )
    ]
    for c in loads:
        c.start()
    loads[0].wait()
    loads[1].wait()
    pl.semaphore_wait(barrier, 31)

    sign = 1 - 2 * (z % 2)
    sends = []

    def shard(o, to):
        slot = near(o)
        c = copy(V.at[slot], V.at[slot], z_send.at[len(sends)], z_recv.at[slot], at_z(near(to)))
        c.start()
        sends.append(c)

    def arrived(*offsets):
        for o in offsets:
            slot = near(o)
            copy(V.at[slot], V.at[slot], z_send.at[0], z_recv.at[slot], at_z(near(1))).wait_recv()

    cot_copy = copy(COT.at[zh], COT.at[zh], c_sem.at[0], c_sem.at[1], at_z(near(8)))
    for o in (5, -5, 2, -2, 1, -1):
        shard(0, o)
    arrived(5, -5)
    shard(-5 * sign, 3 * sign)
    for o in (5, -5):
        for t in (2, -2, 1, -1):
            shard(o, t)
    cot_copy.start()
    arrived(1, -1, 2, -2, 6, -4, -6, 4, 3, -3, 7, -7, 8)
    loads[2].wait()
    loads[3].wait()
    row_ok, col_ok = masks()

    def contribution(p, a):
        plane = V[8 * p : 8 * p + 8].reshape(CHANNELS, FACE)
        taps = W[(a + 1) * 9 * ROWS : (a + 2) * 9 * ROWS, :]
        prod = jnp.dot(taps, plane, preferred_element_type=F32)
        total = None
        for c in (0, -1, 1):
            part = None
            for b in (0, -1, 1):
                i = 3 * (b + 1) + (c + 1)
                term = prod[i * ROWS : (i + 1) * ROWS]
                if b:
                    term = pull(term, BREADTH * b, row_ok[b])
                part = term if part is None else part + term
            if c:
                part = pull(part, c, col_ok[c])
            total = part if total is None else total + part
        return total

    def after(p):
        last = x == 3
        x2 = (x + 1) % 4
        y2 = (y + jnp.where(last, p, 0)) % 4
        return y2 * 4 + x2, jnp.where(last, 1 - p, p)

    def before(p):
        first = x == 0
        x2 = (x + 3) % 4
        y2 = (y + 4 - jnp.where(first, 1 - p, 0)) % 4
        return y2 * 4 + x2, jnp.where(first, 1 - p, p)

    q_copies = []
    for p in (0, 1):
        for side, a, where in ((0, -1, after), (1, 1, before)):
            QS[p, side] = contribution(p, a).astype(BF16)
            j, q = where(p)
            c = copy(QS.at[p, side], QR.at[q, side], q_send.at[p, side], q_recv.at[q, side], at_xy(j))
            c.start()
            q_copies.append(c)
    for p in (0, 1):
        Q0[p] = contribution(p, 0)
    eye = lax.broadcasted_iota(jnp.int32, (ROWS, ROWS), 0) == lax.broadcasted_iota(
        jnp.int32, (ROWS, ROWS), 1
    )
    column = jnp.sum(jnp.where(eye, B[...], 0.0), axis=1, keepdims=True)
    first_plane = (y == 0) & (x == 0)
    last_plane = (y == 3) & (x == 3)
    cot_copy.wait_recv()
    g_copies = []
    bias_total = jnp.zeros((ROWS, 1), F32)
    for p in (0, 1):
        for side in (0, 1):
            copy(
                QS.at[p, side], QR.at[p, side], q_send.at[p, side], q_recv.at[p, side], other
            ).wait_recv()
        before_term = QR[p, 0].astype(F32)
        after_term = QR[p, 1].astype(F32)
        if p == 0:
            before_term = jnp.where(first_plane, 0.0, before_term)
        else:
            after_term = jnp.where(last_plane, 0.0, after_term)
        pre = Q0[p] + before_term + after_term + column
        sig = jax.nn.sigmoid(pre)
        grad = (COT[p].astype(F32) * sig * (1.0 + pre * (1.0 - sig))).astype(BF16)
        GN[p, 1] = grad
        for side, slot, where in ((0, 2, after), (1, 0, before)):
            j, q = where(p)
            c = copy(GN.at[p, 1], GN.at[q, slot], g_send.at[p, side], g_recv.at[q, side], at_xy(j))
            c.start()
            g_copies.append(c)
        ACT[p] = (pre * sig).astype(BF16)
        bias_total = bias_total + jnp.sum(grad.astype(F32), axis=1, keepdims=True)
    act_o[...] = ACT[zh]

    def shifted(p, a):
        grad = GN[p, a + 1].astype(F32)
        if p == 0 and a == 1:
            grad = jnp.where(first_plane, 0.0, grad)
        if p == 1 and a == -1:
            grad = jnp.where(last_plane, 0.0, grad)
        for c in (-1, 0, 1):
            moved = pull(grad, -c, col_ok[-c]) if c else grad
            for b in (-1, 0, 1):
                t = 9 * (a + 1) + 3 * (b + 1) + (c + 1)
                term = pull(moved, -BREADTH * b, row_ok[-b]) if b else moved
                GS[p, t * ROWS : (t + 1) * ROWS, :] = term.astype(BF16)

    def weight_grad(a):
        rows = slice((a + 1) * 9 * ROWS, (a + 2) * 9 * ROWS)
        total = None
        for p in (0, 1):
            plane = V[8 * p : 8 * p + 8].reshape(CHANNELS, FACE)
            term = lax.dot_general(
                GS[p, rows, :], plane, (((1,), (1,)), ((), ())), preferred_element_type=F32
            )
            total = term if total is None else total + term
        for i in range(9):
            t = 9 * (a + 1) + i
            for h in (0, 1):
                piece = total[i * ROWS + h * 16 : i * ROWS + (h + 1) * 16]
                Fp[h, t] = piece
                S[h, t] = piece.astype(BF16)

    for p in (0, 1):
        shifted(p, 0)
    weight_grad(0)
    eye = lax.broadcasted_iota(jnp.int32, (ROWS, CHANNELS), 0) == lax.broadcasted_iota(
        jnp.int32, (ROWS, CHANNELS), 1
    )
    bias_row = jnp.sum(jnp.where(eye, bias_total, 0.0), axis=0, keepdims=True)
    for h in (0, 1):
        Fp[h, TAPS] = jnp.broadcast_to(bias_row, (16, CHANNELS))
        S[h, TAPS] = pack(bias_row)
    for p in (0, 1):
        for side, slot in ((0, 2), (1, 0)):
            copy(
                GN.at[p, 1], GN.at[p, slot], g_send.at[p, side], g_recv.at[p, side], other
            ).wait_recv()
    for a in (-1, 1):
        for p in (0, 1):
            shifted(p, a)
        weight_grad(a)

    d_copy = copy(S.at[1 - d], R0, d_sem.at[0], d_sem.at[1], other)
    d_copy.start()

    part = lax.dot_general(
        W[...], GS[zh], (((0,), (0,)), ((), ())), preferred_element_type=F32
    )
    for i in range(8):
        N[i] = part[i * ROWS : (i + 1) * ROWS].astype(BF16)
    n_copies = []
    for k in range(1, 8):
        to = (f + k) % 8
        c = copy(N.at[to], RG.at[f], n_send.at[k], n_recv.at[f], (d, s, to))
        c.start()
        n_copies.append(c)

    d_copy.wait_recv()
    summed = Fp[d] + R0[...].astype(F32)
    T1[...] = summed.astype(BF16)
    T1[TAPS] = pack(Fp[d, TAPS, 0:1, :] + unpack(R0[TAPS]))

    def mine(ref, j):
        return ref.at[pl.ds(2 * j, 2)]

    def rs_copy(k):
        to = (me + k) % 16
        return to, copy(mine(T1, to), mine(R1, me), rs_send.at[k], rs_recv.at[me], at_xy(to))

    for k in range(1, 16):
        to, c = rs_copy(k)
        pl.when(to < OWNERS)(c.start)

    @pl.when(me < OWNERS)
    def _():
        R1[pl.ds(2 * me, 2)] = T1[pl.ds(2 * me, 2)]
        for k in range(1, 16):
            source = (me + k) % 16
            copy(
                mine(T1, me), mine(R1, source), rs_send.at[k], rs_recv.at[source], at_xy(source)
            ).wait_recv()
        total = R1[0:2].astype(F32)
        for i in range(1, 16):
            total = total + R1[2 * i : 2 * i + 2].astype(F32)
        O[d, pl.ds(2 * me, 2)] = total.astype(BF16)

        @pl.when(me == OWNERS - 1)
        def _():
            O[d, TAPS] = pack(jnp.sum(total[1, 0:2], axis=0, keepdims=True))

        for k in range(1, 16):
            to = (me + k) % 16
            copy(
                O.at[d, pl.ds(2 * me, 2)], O.at[d, pl.ds(2 * me, 2)],
                ag_send.at[k], ag_recv.at[me], at_xy(to),
            ).start()

    own = N[f].astype(F32)
    for k in range(1, 8):
        source = (f + k) % 8
        copy(N.at[source], RG.at[source], n_send.at[k], n_recv.at[source], (d, s, source)).wait_recv()
        own = own + RG[source].astype(F32)
    gin_o[...] = own.astype(BF16)

    for k in range(1, 16):
        source = (me + k) % 16

        @pl.when(source < OWNERS)
        def _():
            copy(
                O.at[d, pl.ds(2 * source, 2)], O.at[d, pl.ds(2 * source, 2)],
                ag_send.at[k], ag_recv.at[source], at_xy(source),
            ).wait_recv()

    e_copy = copy(O.at[d], O.at[d], e_sem.at[0], e_sem.at[1], other)
    e_copy.start()

    def finish(h):
        gw_o[:, pl.ds(pl.multiple_of(h * 16, 16), 16), :] = O[h, 0:TAPS].astype(F32) * scale

    finish(d)
    copy(O.at[1 - d], O.at[1 - d], e_sem.at[0], e_sem.at[1], other).wait_recv()
    finish(1 - d)
    gb_o[...] = unpack(O[0, TAPS])[:, :ROWS] * scale

    for c in sends + q_copies + g_copies + n_copies + [cot_copy, d_copy, e_copy]:
        c.wait_send()
    for k in range(1, 16):
        to, c = rs_copy(k)
        pl.when(to < OWNERS)(c.wait_send)

    @pl.when(me < OWNERS)
    def _():
        for k in range(1, 16):
            to = (me + k) % 16
            copy(
                O.at[d, pl.ds(2 * me, 2)], O.at[d, pl.ds(2 * me, 2)],
                ag_send.at[k], ag_recv.at[me], at_xy(to),
            ).wait_send()


def store(act, gin, gw, gb, act_o, gin_o, gw_o, gb_o, sem):
    copies = [
        pltpu.make_async_copy(src, dst, sem.at[i])
        for i, (src, dst) in enumerate(((gw, gw_o), (act, act_o), (gin, gin_o), (gb, gb_o)))
    ]
    for c in copies:
        c.start()
    for c in copies:
        c.wait()


def per_device(scale, volumes, weight, bias, cotangent):
    vmem = pl.BlockSpec(memory_space=pltpu.VMEM)
    hbm = pl.BlockSpec(memory_space=pltpu.HBM)
    dma = pltpu.SemaphoreType.DMA
    act, gin, gw, gb = pl.pallas_call(
        functools.partial(kernel, scale),
        out_shape=[
            pltpu.VMEM((ROWS, FACE), BF16),
            pltpu.VMEM((ROWS, FACE), BF16),
            pltpu.VMEM((TAPS, ROWS, CHANNELS), F32),
            pltpu.VMEM((1, ROWS), F32),
        ],
        in_specs=[hbm] * 4,
        out_specs=[vmem] * 4,
        scratch_shapes=[
            pltpu.VMEM((16, ROWS, FACE), BF16),
            pltpu.VMEM((2, ROWS, FACE), BF16),
            pltpu.VMEM((2, 2, ROWS, FACE), BF16),
            pltpu.VMEM((2, 2, ROWS, FACE), BF16),
            pltpu.VMEM((2, ROWS, FACE), F32),
            pltpu.VMEM((2, ROWS, FACE), BF16),
            pltpu.VMEM((2, 3, ROWS, FACE), BF16),
            pltpu.VMEM((2, TAPS * ROWS, FACE), BF16),
            pltpu.VMEM((2, UNITS, 16, CHANNELS), F32),
            pltpu.VMEM((2, UNITS, 16, CHANNELS), BF16),
            pltpu.VMEM((UNITS, 16, CHANNELS), BF16),
            pltpu.VMEM((UNITS, 16, CHANNELS), BF16),
            pltpu.VMEM((32, 16, CHANNELS), BF16),
            pltpu.VMEM((2, UNITS, 16, CHANNELS), BF16),
            pltpu.VMEM((8, ROWS, FACE), BF16),
            pltpu.VMEM((8, ROWS, FACE), BF16),
            pltpu.VMEM((TAPS * ROWS, CHANNELS), BF16),
            pltpu.VMEM((1, ROWS), F32),
            dma((4,)), dma((15,)), dma((16,)), dma((2,)),
            dma((2, 2)), dma((2, 2)), dma((2, 2)), dma((2, 2)),
            dma((2,)), dma((16,)), dma((16,)), dma((16,)), dma((16,)), dma((2,)),
            dma((8,)), dma((8,)),
        ],
        compiler_params=pltpu.CompilerParams(
            collective_id=0, has_side_effects=True, vmem_limit_bytes=48 * 2**20
        ),
    )(
        *(
            pltpu.with_memory_space_constraint(a, pltpu.HBM)
            for a in (
                volumes.reshape(ROWS, FACE),
                weight.reshape(TAPS * ROWS, CHANNELS),
                bias.reshape(1, ROWS),
                cotangent.reshape(ROWS, FACE),
            )
        )
    )
    act, gin, gw, gb = pl.pallas_call(
        store,
        out_shape=[
            jax.ShapeDtypeStruct((ROWS, FACE), BF16),
            jax.ShapeDtypeStruct((ROWS, FACE), BF16),
            jax.ShapeDtypeStruct((TAPS, ROWS, CHANNELS), F32),
            jax.ShapeDtypeStruct((1, ROWS), F32),
        ],
        in_specs=[vmem] * 4,
        out_specs=[hbm] * 4,
        scratch_shapes=[dma((4,))],
    )(*(pltpu.with_memory_space_constraint(a, pltpu.VMEM) for a in (act, gin, gw, gb)))
    shape = (1, ROWS, 1, FACE)
    return act.reshape(shape), gin.reshape(shape), gw, gb.reshape(ROWS)


def solution(mesh):
    scale = 1.0 / math.sqrt(2 * 32 * FACE)
    return jax.shard_map(
        functools.partial(per_device, scale),
        mesh=mesh,
        in_specs=(
            P("dp", "filter", "space", None),
            P(None, "filter", None),
            P("filter"),
            P("dp", "filter", "space", None),
        ),
        out_specs=(
            P("dp", "filter", "space", None),
            P("dp", "filter", "space", None),
            P(None, "filter", None),
            P("filter"),
        ),
        check_vma=False,
    )
```

```python
import functools
import math

import jax
import jax.numpy as jnp
from jax import lax
from jax.experimental import pallas as pl
from jax.experimental.pallas import tpu as pltpu
from jax.sharding import PartitionSpec as P

HEIGHT = 16
BREADTH = 32
FACE = HEIGHT * BREADTH
ROWS = 32
CHANNELS = 256
TAPS = 27
UNITS = 28
OWNERS = UNITS // 2
MESH = pl.DeviceIdType.MESH
F32 = jnp.float32
BF16 = jnp.bfloat16
SHIFTS = [(b, c) for b in (-1, 0, 1) for c in (-1, 0, 1)]


def masks():
    f = lax.broadcasted_iota(jnp.int32, (ROWS, FACE), 1)
    row, col = f // BREADTH, f % BREADTH
    row_ok = {b: (row + b >= 0) & (row + b < HEIGHT) for b in (-1, 1)}
    col_ok = {c: (col + c >= 0) & (col + c < BREADTH) for c in (-1, 1)}
    return row_ok, col_ok


def pull(x, amount, ok):
    return jnp.where(ok, pltpu.roll(x, (-amount) % FACE, 1), 0.0)


def pack(v):
    high = v.astype(BF16).astype(F32)
    low = v - high
    row = lax.broadcasted_iota(jnp.int32, (16, CHANNELS), 0)
    return jnp.where(row == 0, high, jnp.where(row == 1, low, 0.0)).astype(BF16)


def unpack(unit):
    u = unit.astype(F32)
    row = lax.broadcasted_iota(jnp.int32, u.shape, 0)
    return jnp.sum(jnp.where(row < 2, u, 0.0), axis=0, keepdims=True)


def kernel(
    scale,
    vol, w, bias, cot,
    act_o, gin_o, gw_o, gb_o,
    V, COT, ACT, GN, GS, Fp, S, R0, T1, R1, O, N, RG, W, WT, B,
    in_sem, z_send, z_recv, x_send, x_recv, c_sem, g_send, g_recv,
    d_sem, rs_send, rs_recv, ag_send, ag_recv, e_sem, n_send, n_recv,
):
    d = lax.axis_index("dp")
    s = lax.axis_index("space")
    f = lax.axis_index("filter")
    y = s // 8
    zh = (s // 4) % 2
    x = s % 4
    z = zh * 8 + f
    me = y * 4 + x
    sign = 1 - 2 * (z % 2)

    def at_z(k):
        return (d, y * 8 + (k // 8) * 4 + x, k % 8)

    def at_xy(j):
        return (d, (j // 4) * 8 + zh * 4 + j % 4, f)

    def near(k):
        return (z + k + 16) % 16

    other = (1 - d, s, f)

    def copy(src, dst, send, recv, to):
        return pltpu.make_async_remote_copy(
            src_ref=src, dst_ref=dst, send_sem=send, recv_sem=recv,
            device_id=to, device_id_type=MESH,
        )

    barrier = pltpu.get_barrier_semaphore()
    for k in range(1, 16):
        pl.semaphore_signal(barrier, inc=1, device_id=at_z((z + k) % 16), device_id_type=MESH)
        pl.semaphore_signal(barrier, inc=1, device_id=at_xy((me + k) % 16), device_id_type=MESH)
    pl.semaphore_signal(barrier, inc=1, device_id=other, device_id_type=MESH)
    loads = [
        pltpu.make_async_copy(src, dst, in_sem.at[i])
        for i, (src, dst) in enumerate(
            ((vol, V.at[zh, 1, f]), (cot, COT.at[zh]), (w, W), (bias, B))
        )
    ]
    for c in loads:
        c.start()
    loads[0].wait()
    loads[1].wait()
    pl.semaphore_wait(barrier, 31)

    def after(p):
        last = x == 3
        x2 = (x + 1) % 4
        y2 = (y + jnp.where(last, p, 0)) % 4
        return y2 * 4 + x2, jnp.where(last, 1 - p, p)

    def before(p):
        first = x == 0
        x2 = (x + 3) % 4
        y2 = (y + 4 - jnp.where(first, 1 - p, 0)) % 4
        return y2 * 4 + x2, jnp.where(first, 1 - p, p)

    sends = []
    x_copies = []

    def place(slot):
        return V.at[slot // 8, 1, slot % 8]

    def shard(o, to):
        slot = near(o)
        c = copy(place(slot), place(slot), z_send.at[len(sends)], z_recv.at[slot], at_z(near(to)))
        c.start()
        sends.append(c)

    def beside(*offsets):
        for o in offsets:
            slot = near(o)
            p, i = slot // 8, slot % 8
            for side, where in ((0, after), (2, before)):
                j, q = where(p)
                c = copy(
                    place(slot), V.at[q, side, i],
                    x_send.at[len(x_copies)], x_recv.at[q, side // 2, i], at_xy(j),
                )
                c.start()
                x_copies.append(c)

    def arrived(*offsets):
        for o in offsets:
            slot = near(o)
            copy(place(slot), place(slot), z_send.at[0], z_recv.at[slot], at_z(near(1))).wait_recv()

    cot_copy = copy(COT.at[zh], COT.at[zh], c_sem.at[0], c_sem.at[1], at_z(near(8)))
    for o in (3, -3, 1, -1):
        shard(0, o)
    beside(0)
    loads[2].wait()
    loads[3].wait()
    WT[...] = W[...].T
    for o in (1, -1):
        arrived(o)
        beside(o)
    for o in (3, -3):
        arrived(o)
        for t in (-o, 1, -1):
            shard(o, t)
    beside(3, -3)

    for o in (2, -2):
        arrived(o)
        beside(o)
    for o in (6, -6):
        arrived(o)
        for t in (1, -1):
            shard(o, t)
    for o in (4, -4):
        arrived(o)
        beside(o)
    beside(6, -6)
    cot_copy.start()
    for o in (5, -5):
        arrived(o)
        beside(o)
    arrived(-7 * sign)
    shard(-7 * sign, sign)
    beside(-7 * sign)
    for o in (7 * sign, 8):
        arrived(o)
        beside(o)
    for p in (0, 1):
        for side in (0, 2):
            for i in range(8):
                copy(
                    V.at[p, side, i], V.at[p, side, i],
                    x_send.at[0], x_recv.at[p, side // 2, i], at_xy((me + 1) % 16),
                ).wait_recv()

    first_plane = (y == 0) & (x == 0)
    last_plane = (y == 3) & (x == 3)

    @pl.when(first_plane)
    def _():
        V[0, 0] = jnp.zeros((8, ROWS, FACE), BF16)

    @pl.when(last_plane)
    def _():
        V[1, 2] = jnp.zeros((8, ROWS, FACE), BF16)

    row_ok, col_ok = masks()
    eye = lax.broadcasted_iota(jnp.int32, (ROWS, ROWS), 0) == lax.broadcasted_iota(
        jnp.int32, (ROWS, ROWS), 1
    )
    column = jnp.sum(jnp.where(eye, B[...], 0.0), axis=1, keepdims=True)

    def pre_activation(p):
        taps = jnp.concatenate([W[a * 9 * ROWS : (a + 1) * 9 * ROWS] for a in range(3)], axis=1)
        planes = V[p].reshape(3 * CHANNELS, FACE)
        prod = jnp.dot(taps, planes, preferred_element_type=F32)
        total = column
        for c in (0, -1, 1):
            part = None
            for b in (0, -1, 1):
                i = 3 * (b + 1) + (c + 1)
                term = prod[i * ROWS : (i + 1) * ROWS]
                if b:
                    term = pull(term, BREADTH * b, row_ok[b])
                part = term if part is None else part + term
            if c:
                part = pull(part, c, col_ok[c])
            total = total + part
        return total

    def shifted(p, a, grad):
        for c in (-1, 0, 1):
            moved = pull(grad, -c, col_ok[-c]) if c else grad
            for b in (-1, 0, 1):
                i = 3 * (b + 1) + (c + 1)
                term = pull(moved, -BREADTH * b, row_ok[-b]) if b else moved
                GS[p, a + 1, i * ROWS : (i + 1) * ROWS, :] = term.astype(BF16)

    cot_copy.wait_recv()
    g_copies = []
    bias_total = jnp.zeros((ROWS, 1), F32)
    for p in (0, 1):
        pre = pre_activation(p)
        sig = jax.nn.sigmoid(pre)
        grad = (COT[p].astype(F32) * sig * (1.0 + pre * (1.0 - sig))).astype(BF16)
        GN[p, 1] = grad
        for side, slot, where in ((0, 2, after), (1, 0, before)):
            j, q = where(p)
            c = copy(GN.at[p, 1], GN.at[q, slot], g_send.at[p, side], g_recv.at[q, side], at_xy(j))
            c.start()
            g_copies.append(c)
        ACT[p] = (pre * sig).astype(BF16)
        grad = grad.astype(F32)
        bias_total = bias_total + jnp.sum(grad, axis=1, keepdims=True)
        shifted(p, 0, grad)

    total = None
    for p in (0, 1):
        term = lax.dot_general(
            GS[p, 1], V[p].reshape(3 * CHANNELS, FACE),
            (((1,), (1,)), ((), ())), preferred_element_type=F32,
        )
        total = term if total is None else total + term
    for a in range(3):
        for i in range(9):
            for h in (0, 1):
                piece = total[
                    i * ROWS + h * 16 : i * ROWS + (h + 1) * 16,
                    a * CHANNELS : (a + 1) * CHANNELS,
                ]
                Fp[h, 9 * a + i] = piece
                S[h, 9 * a + i] = piece.astype(BF16)
    eye = lax.broadcasted_iota(jnp.int32, (ROWS, CHANNELS), 0) == lax.broadcasted_iota(
        jnp.int32, (ROWS, CHANNELS), 1
    )
    bias_row = jnp.sum(jnp.where(eye, bias_total, 0.0), axis=0, keepdims=True)
    for h in (0, 1):
        Fp[h, TAPS] = jnp.broadcast_to(bias_row, (16, CHANNELS))
        S[h, TAPS] = pack(bias_row)

    d_copy = copy(S.at[1 - d], R0, d_sem.at[0], d_sem.at[1], other)
    d_copy.start()
    act_o[...] = ACT[zh]
    d_copy.wait_recv()
    summed = Fp[d] + R0[...].astype(F32)
    T1[...] = summed.astype(BF16)
    T1[TAPS] = pack(Fp[d, TAPS, 0:1, :] + unpack(R0[TAPS]))

    def mine(ref, j):
        return ref.at[pl.ds(2 * j, 2)]

    def rs_copy(k):
        to = (me + k) % 16
        return to, copy(mine(T1, to), mine(R1, me), rs_send.at[k], rs_recv.at[me], at_xy(to))

    for k in range(1, 16):
        to, c = rs_copy(k)
        pl.when(to < OWNERS)(c.start)

    for p in (0, 1):
        for side, slot in ((0, 2), (1, 0)):
            copy(
                GN.at[p, 1], GN.at[p, slot], g_send.at[p, side], g_recv.at[p, side], other
            ).wait_recv()
    for p in (0, 1):
        for a in (-1, 1):
            grad = GN[p, a + 1].astype(F32)
            if p == 0 and a == 1:
                grad = jnp.where(first_plane, 0.0, grad)
            if p == 1 and a == -1:
                grad = jnp.where(last_plane, 0.0, grad)
            shifted(p, a, grad)
        part = jnp.dot(
            WT[...], GS[p].reshape(TAPS * ROWS, FACE), preferred_element_type=F32
        )
        for i in range(8):
            N[p, i] = part[i * ROWS : (i + 1) * ROWS].astype(BF16)
    n_copies = []
    for i, o in enumerate((-4 * sign, 3, -3, 2, -2, 1, -1)):
        to = near(o)
        c = copy(N.at[to // 8, to % 8], RG.at[i], n_send.at[i], n_recv.at[i], at_z(to))
        c.start()
        n_copies.append(c)

    @pl.when(me < OWNERS)
    def _():
        R1[pl.ds(2 * me, 2)] = T1[pl.ds(2 * me, 2)]
        for k in range(1, 16):
            source = (me + k) % 16
            copy(
                mine(T1, me), mine(R1, source), rs_send.at[k], rs_recv.at[source], at_xy(source)
            ).wait_recv()
        total = R1[0:2].astype(F32)
        for i in range(1, 16):
            total = total + R1[2 * i : 2 * i + 2].astype(F32)
        O[d, pl.ds(2 * me, 2)] = total.astype(BF16)

        @pl.when(me == OWNERS - 1)
        def _():
            O[d, TAPS] = pack(jnp.sum(total[1, 0:2], axis=0, keepdims=True))

        for k in range(1, 16):
            to = (me + k) % 16
            copy(
                O.at[d, pl.ds(2 * me, 2)], O.at[d, pl.ds(2 * me, 2)],
                ag_send.at[k], ag_recv.at[me], at_xy(to),
            ).start()

    for k in range(1, 16):
        source = (me + k) % 16

        @pl.when(source < OWNERS)
        def _():
            copy(
                O.at[d, pl.ds(2 * source, 2)], O.at[d, pl.ds(2 * source, 2)],
                ag_send.at[k], ag_recv.at[source], at_xy(source),
            ).wait_recv()

    e_copy = copy(O.at[d], O.at[d], e_sem.at[0], e_sem.at[1], other)
    e_copy.start()

    def finish(h):
        gw_o[:, pl.ds(pl.multiple_of(h * 16, 16), 16), :] = O[h, 0:TAPS].astype(F32) * scale

    finish(d)
    own = N[zh, f].astype(F32)
    for c in n_copies:
        c.wait_recv()
    for i in range(7):
        own = own + RG[i].astype(F32)
    gin_o[...] = own.astype(BF16)
    copy(O.at[1 - d], O.at[1 - d], e_sem.at[0], e_sem.at[1], other).wait_recv()
    finish(1 - d)
    gb_o[...] = unpack(O[0, TAPS])[:, :ROWS] * scale

    for c in sends + x_copies + g_copies + n_copies + [cot_copy, d_copy, e_copy]:
        c.wait_send()
    for k in range(1, 16):
        to, c = rs_copy(k)
        pl.when(to < OWNERS)(c.wait_send)

    @pl.when(me < OWNERS)
    def _():
        for k in range(1, 16):
            to = (me + k) % 16
            copy(
                O.at[d, pl.ds(2 * me, 2)], O.at[d, pl.ds(2 * me, 2)],
                ag_send.at[k], ag_recv.at[me], at_xy(to),
            ).wait_send()


def store(act, gin, gw, gb, act_o, gin_o, gw_o, gb_o, sem):
    copies = [
        pltpu.make_async_copy(src, dst, sem.at[i])
        for i, (src, dst) in enumerate(((gw, gw_o), (act, act_o), (gin, gin_o), (gb, gb_o)))
    ]
    for c in copies:
        c.start()
    for c in copies:
        c.wait()


def per_device(scale, volumes, weight, bias, cotangent):
    vmem = pl.BlockSpec(memory_space=pltpu.VMEM)
    hbm = pl.BlockSpec(memory_space=pltpu.HBM)
    dma = pltpu.SemaphoreType.DMA
    act, gin, gw, gb = pl.pallas_call(
        functools.partial(kernel, scale),
        out_shape=[
            pltpu.VMEM((ROWS, FACE), BF16),
            pltpu.VMEM((ROWS, FACE), BF16),
            pltpu.VMEM((TAPS, ROWS, CHANNELS), F32),
            pltpu.VMEM((1, ROWS), F32),
        ],
        in_specs=[hbm] * 4,
        out_specs=[vmem] * 4,
        scratch_shapes=[
            pltpu.VMEM((2, 3, 8, ROWS, FACE), BF16),
            pltpu.VMEM((2, ROWS, FACE), BF16),
            pltpu.VMEM((2, ROWS, FACE), BF16),
            pltpu.VMEM((2, 3, ROWS, FACE), BF16),
            pltpu.VMEM((2, 3, 9 * ROWS, FACE), BF16),
            pltpu.VMEM((2, UNITS, 16, CHANNELS), F32),
            pltpu.VMEM((2, UNITS, 16, CHANNELS), BF16),
            pltpu.VMEM((UNITS, 16, CHANNELS), BF16),
            pltpu.VMEM((UNITS, 16, CHANNELS), BF16),
            pltpu.VMEM((32, 16, CHANNELS), BF16),
            pltpu.VMEM((2, UNITS, 16, CHANNELS), BF16),
            pltpu.VMEM((2, 8, ROWS, FACE), BF16),
            pltpu.VMEM((7, ROWS, FACE), BF16),
            pltpu.VMEM((TAPS * ROWS, CHANNELS), BF16),
            pltpu.VMEM((CHANNELS, TAPS * ROWS), BF16),
            pltpu.VMEM((1, ROWS), F32),
            dma((4,)), dma((15,)), dma((16,)), dma((32,)), dma((2, 2, 8)), dma((2,)),
            dma((2, 2)), dma((2, 2)),
            dma((2,)), dma((16,)), dma((16,)), dma((16,)), dma((16,)), dma((2,)),
            dma((7,)), dma((7,)),
        ],
        compiler_params=pltpu.CompilerParams(
            collective_id=0, has_side_effects=True, vmem_limit_bytes=48 * 2**20
        ),
    )(
        *(
            pltpu.with_memory_space_constraint(a, pltpu.HBM)
            for a in (
                volumes.reshape(ROWS, FACE),
                weight.reshape(TAPS * ROWS, CHANNELS),
                bias.reshape(1, ROWS),
                cotangent.reshape(ROWS, FACE),
            )
        )
    )
    act, gin, gw, gb = pl.pallas_call(
        store,
        out_shape=[
            jax.ShapeDtypeStruct((ROWS, FACE), BF16),
            jax.ShapeDtypeStruct((ROWS, FACE), BF16),
            jax.ShapeDtypeStruct((TAPS, ROWS, CHANNELS), F32),
            jax.ShapeDtypeStruct((1, ROWS), F32),
        ],
        in_specs=[vmem] * 4,
        out_specs=[hbm] * 4,
        scratch_shapes=[dma((4,))],
    )(*(pltpu.with_memory_space_constraint(a, pltpu.VMEM) for a in (act, gin, gw, gb)))
    shape = (1, ROWS, 1, FACE)
    return act.reshape(shape), gin.reshape(shape), gw, gb.reshape(ROWS)


def solution(mesh):
    scale = 1.0 / math.sqrt(2 * 32 * FACE)
    return jax.shard_map(
        functools.partial(per_device, scale),
        mesh=mesh,
        in_specs=(
            P("dp", "filter", "space", None),
            P(None, "filter", None),
            P("filter"),
            P("dp", "filter", "space", None),
        ),
        out_specs=(
            P("dp", "filter", "space", None),
            P("dp", "filter", "space", None),
            P(None, "filter", None),
            P("filter"),
        ),
        check_vma=False,
    )
```

```python
import functools
import math

import jax
import jax.numpy as jnp
from jax import lax
from jax.experimental import pallas as pl
from jax.experimental.pallas import tpu as pltpu
from jax.sharding import PartitionSpec as P

HEIGHT = 16
BREADTH = 32
FACE = HEIGHT * BREADTH
ROWS = 32
CHANNELS = 256
TAPS = 27
UNITS = 28
OWNERS = UNITS // 2
MESH = pl.DeviceIdType.MESH
F32 = jnp.float32
BF16 = jnp.bfloat16
SHIFTS = [(b, c) for b in (-1, 0, 1) for c in (-1, 0, 1)]


def masks():
    f = lax.broadcasted_iota(jnp.int32, (ROWS, FACE), 1)
    row, col = f // BREADTH, f % BREADTH
    row_ok = {b: (row + b >= 0) & (row + b < HEIGHT) for b in (-1, 1)}
    col_ok = {c: (col + c >= 0) & (col + c < BREADTH) for c in (-1, 1)}
    return row_ok, col_ok


def pull(x, amount, ok):
    return jnp.where(ok, pltpu.roll(x, (-amount) % FACE, 1), 0.0)


def pack(v):
    high = v.astype(BF16).astype(F32)
    low = v - high
    row = lax.broadcasted_iota(jnp.int32, (16, CHANNELS), 0)
    return jnp.where(row == 0, high, jnp.where(row == 1, low, 0.0)).astype(BF16)


def unpack(unit):
    u = unit.astype(F32)
    row = lax.broadcasted_iota(jnp.int32, u.shape, 0)
    return jnp.sum(jnp.where(row < 2, u, 0.0), axis=0, keepdims=True)


def kernel(
    scale,
    vol, w, bias, cot,
    act_o, gin_o, gw_o, gb_o,
    V, COT, ACT, GN, GS, Fp, S, R0, T1, R1, O, N, RG, W, WT, B,
    in_sem, z_send, z_recv, x_send, x_recv, c_sem, g_send, g_recv,
    d_sem, rs_send, rs_recv, ag_send, ag_recv, e_sem, n_send, n_recv,
):
    d = lax.axis_index("dp")
    s = lax.axis_index("space")
    f = lax.axis_index("filter")
    y = s // 8
    zh = (s // 4) % 2
    x = s % 4
    z = zh * 8 + f
    me = y * 4 + x
    sign = 1 - 2 * (z % 2)

    def at_z(k):
        return (d, y * 8 + (k // 8) * 4 + x, k % 8)

    def at_xy(j):
        return (d, (j // 4) * 8 + zh * 4 + j % 4, f)

    def near(k):
        return (z + k + 16) % 16

    other = (1 - d, s, f)

    def copy(src, dst, send, recv, to):
        return pltpu.make_async_remote_copy(
            src_ref=src, dst_ref=dst, send_sem=send, recv_sem=recv,
            device_id=to, device_id_type=MESH,
        )

    barrier = pltpu.get_barrier_semaphore()
    for k in range(1, 16):
        pl.semaphore_signal(barrier, inc=1, device_id=at_z((z + k) % 16), device_id_type=MESH)
        pl.semaphore_signal(barrier, inc=1, device_id=at_xy((me + k) % 16), device_id_type=MESH)
    pl.semaphore_signal(barrier, inc=1, device_id=other, device_id_type=MESH)
    loads = [
        pltpu.make_async_copy(src, dst, in_sem.at[i])
        for i, (src, dst) in enumerate(
            ((vol, V.at[zh, 1, f]), (cot, COT.at[zh]), (w, W), (bias, B))
        )
    ]
    for c in loads:
        c.start()
    loads[0].wait()
    loads[1].wait()
    pl.semaphore_wait(barrier, 31)

    def after(p):
        last = x == 3
        x2 = (x + 1) % 4
        y2 = (y + jnp.where(last, p, 0)) % 4
        return y2 * 4 + x2, jnp.where(last, 1 - p, p)

    def before(p):
        first = x == 0
        x2 = (x + 3) % 4
        y2 = (y + 4 - jnp.where(first, 1 - p, 0)) % 4
        return y2 * 4 + x2, jnp.where(first, 1 - p, p)

    sends = []
    x_copies = []

    def place(slot):
        return V.at[slot // 8, 1, slot % 8]

    def shard(o, to):
        slot = near(o)
        c = copy(place(slot), place(slot), z_send.at[len(sends)], z_recv.at[slot], at_z(near(to)))
        c.start()
        sends.append(c)

    def beside(*offsets):
        for o in offsets:
            slot = near(o)
            p, i = slot // 8, slot % 8
            for side, where in ((0, after), (2, before)):
                j, q = where(p)
                c = copy(
                    place(slot), V.at[q, side, i],
                    x_send.at[len(x_copies)], x_recv.at[q, side // 2, i], at_xy(j),
                )
                c.start()
                x_copies.append(c)

    def arrived(*offsets):
        for o in offsets:
            slot = near(o)
            copy(place(slot), place(slot), z_send.at[0], z_recv.at[slot], at_z(near(1))).wait_recv()

    cot_copy = copy(COT.at[zh], COT.at[zh], c_sem.at[0], c_sem.at[1], at_z(near(8)))
    for o in (3, -3, 1, -1):
        shard(0, o)
    beside(0)
    loads[2].wait()
    loads[3].wait()
    WT[...] = W[...].T
    for o in (1, -1):
        arrived(o)
        beside(o)
    for o in (3, -3):
        arrived(o)
        for t in (-o, 1, -1):
            shard(o, t)
    beside(3, -3)
    for o in (2, -2, 4, -4):
        arrived(o)
        beside(o)
    for o in (6, -6):
        arrived(o)
        for t in (1, -1):
            shard(o, t)
    shard(-6 * sign, 2 * sign)
    beside(6, -6)
    cot_copy.start()
    for o in (5, -5, 7, -7, 8):
        arrived(o)
        beside(o)
    for p in (0, 1):
        for side in (0, 2):
            for i in range(8):
                copy(
                    V.at[p, side, i], V.at[p, side, i],
                    x_send.at[0], x_recv.at[p, side // 2, i], at_xy((me + 1) % 16),
                ).wait_recv()

    first_plane = (y == 0) & (x == 0)
    last_plane = (y == 3) & (x == 3)

    @pl.when(first_plane)
    def _():
        V[0, 0] = jnp.zeros((8, ROWS, FACE), BF16)

    @pl.when(last_plane)
    def _():
        V[1, 2] = jnp.zeros((8, ROWS, FACE), BF16)

    row_ok, col_ok = masks()
    eye = lax.broadcasted_iota(jnp.int32, (ROWS, ROWS), 0) == lax.broadcasted_iota(
        jnp.int32, (ROWS, ROWS), 1
    )
    column = jnp.sum(jnp.where(eye, B[...], 0.0), axis=1, keepdims=True)

    def pre_activation(p):
        taps = jnp.concatenate([W[a * 9 * ROWS : (a + 1) * 9 * ROWS] for a in range(3)], axis=1)
        planes = V[p].reshape(3 * CHANNELS, FACE)
        prod = jnp.dot(taps, planes, preferred_element_type=F32)
        total = column
        for c in (0, -1, 1):
            part = None
            for b in (0, -1, 1):
                i = 3 * (b + 1) + (c + 1)
                term = prod[i * ROWS : (i + 1) * ROWS]
                if b:
                    term = pull(term, BREADTH * b, row_ok[b])
                part = term if part is None else part + term
            if c:
                part = pull(part, c, col_ok[c])
            total = total + part
        return total

    def shifted(p, a, grad):
        for c in (-1, 0, 1):
            moved = pull(grad, -c, col_ok[-c]) if c else grad
            for b in (-1, 0, 1):
                i = 3 * (b + 1) + (c + 1)
                term = pull(moved, -BREADTH * b, row_ok[-b]) if b else moved
                GS[p, a + 1, i * ROWS : (i + 1) * ROWS, :] = term.astype(BF16)

    cot_copy.wait_recv()
    g_copies = []
    bias_total = jnp.zeros((ROWS, 1), F32)
    for p in (0, 1):
        pre = pre_activation(p)
        sig = jax.nn.sigmoid(pre)
        grad = (COT[p].astype(F32) * sig * (1.0 + pre * (1.0 - sig))).astype(BF16)
        GN[p, 1] = grad
        for side, slot, where in ((0, 2, after), (1, 0, before)):
            j, q = where(p)
            c = copy(GN.at[p, 1], GN.at[q, slot], g_send.at[p, side], g_recv.at[q, side], at_xy(j))
            c.start()
            g_copies.append(c)
        ACT[p] = (pre * sig).astype(BF16)
        grad = grad.astype(F32)
        bias_total = bias_total + jnp.sum(grad, axis=1, keepdims=True)
        shifted(p, 0, grad)

    total = None
    for p in (0, 1):
        term = lax.dot_general(
            GS[p, 1], V[p].reshape(3 * CHANNELS, FACE),
            (((1,), (1,)), ((), ())), preferred_element_type=F32,
        )
        total = term if total is None else total + term
    for a in range(3):
        for i in range(9):
            for h in (0, 1):
                piece = total[
                    i * ROWS + h * 16 : i * ROWS + (h + 1) * 16,
                    a * CHANNELS : (a + 1) * CHANNELS,
                ]
                Fp[h, 9 * a + i] = piece
                S[h, 9 * a + i] = piece.astype(BF16)
    eye = lax.broadcasted_iota(jnp.int32, (ROWS, CHANNELS), 0) == lax.broadcasted_iota(
        jnp.int32, (ROWS, CHANNELS), 1
    )
    bias_row = jnp.sum(jnp.where(eye, bias_total, 0.0), axis=0, keepdims=True)
    for h in (0, 1):
        Fp[h, TAPS] = jnp.broadcast_to(bias_row, (16, CHANNELS))
        S[h, TAPS] = pack(bias_row)

    d_copy = copy(S.at[1 - d], R0, d_sem.at[0], d_sem.at[1], other)
    d_copy.start()
    act_o[...] = ACT[zh]
    d_copy.wait_recv()
    summed = Fp[d] + R0[...].astype(F32)
    T1[...] = summed.astype(BF16)
    T1[TAPS] = pack(Fp[d, TAPS, 0:1, :] + unpack(R0[TAPS]))

    def mine(ref, j):
        return ref.at[pl.ds(2 * j, 2)]

    def rs_copy(k):
        to = (me + k) % 16
        return to, copy(mine(T1, to), mine(R1, me), rs_send.at[k], rs_recv.at[me], at_xy(to))

    for k in range(1, 16):
        to, c = rs_copy(k)
        pl.when(to < OWNERS)(c.start)

    for p in (0, 1):
        for side, slot in ((0, 2), (1, 0)):
            copy(
                GN.at[p, 1], GN.at[p, slot], g_send.at[p, side], g_recv.at[p, side], other
            ).wait_recv()
    for p in (0, 1):
        for a in (-1, 1):
            grad = GN[p, a + 1].astype(F32)
            if p == 0 and a == 1:
                grad = jnp.where(first_plane, 0.0, grad)
            if p == 1 and a == -1:
                grad = jnp.where(last_plane, 0.0, grad)
            shifted(p, a, grad)
        part = jnp.dot(
            WT[...], GS[p].reshape(TAPS * ROWS, FACE), preferred_element_type=F32
        )
        for i in range(8):
            N[p, i] = part[i * ROWS : (i + 1) * ROWS].astype(BF16)
    n_copies = []
    for i, o in enumerate((-4 * sign, 3, -3, 2, -2, 1, -1)):
        to = near(o)
        c = copy(N.at[to // 8, to % 8], RG.at[i], n_send.at[i], n_recv.at[i], at_z(to))
        c.start()
        n_copies.append(c)

    @pl.when(me < OWNERS)
    def _():
        R1[pl.ds(2 * me, 2)] = T1[pl.ds(2 * me, 2)]
        for k in range(1, 16):
            source = (me + k) % 16
            copy(
                mine(T1, me), mine(R1, source), rs_send.at[k], rs_recv.at[source], at_xy(source)
            ).wait_recv()
        total = R1[0:2].astype(F32)
        for i in range(1, 16):
            total = total + R1[2 * i : 2 * i + 2].astype(F32)
        O[d, pl.ds(2 * me, 2)] = total.astype(BF16)

        @pl.when(me == OWNERS - 1)
        def _():
            O[d, TAPS] = pack(jnp.sum(total[1, 0:2], axis=0, keepdims=True))

        for k in range(1, 16):
            to = (me + k) % 16
            copy(
                O.at[d, pl.ds(2 * me, 2)], O.at[d, pl.ds(2 * me, 2)],
                ag_send.at[k], ag_recv.at[me], at_xy(to),
            ).start()

    for k in range(1, 16):
        source = (me + k) % 16

        @pl.when(source < OWNERS)
        def _():
            copy(
                O.at[d, pl.ds(2 * source, 2)], O.at[d, pl.ds(2 * source, 2)],
                ag_send.at[k], ag_recv.at[source], at_xy(source),
            ).wait_recv()

    e_copy = copy(O.at[d], O.at[d], e_sem.at[0], e_sem.at[1], other)
    e_copy.start()

    def finish(h):
        gw_o[:, pl.ds(pl.multiple_of(h * 16, 16), 16), :] = O[h, 0:TAPS].astype(F32) * scale

    finish(d)
    own = N[zh, f].astype(F32)
    for c in n_copies:
        c.wait_recv()
    for i in range(7):
        own = own + RG[i].astype(F32)
    gin_o[...] = own.astype(BF16)
    copy(O.at[1 - d], O.at[1 - d], e_sem.at[0], e_sem.at[1], other).wait_recv()
    finish(1 - d)
    gb_o[...] = unpack(O[0, TAPS])[:, :ROWS] * scale

    for c in sends + x_copies + g_copies + n_copies + [cot_copy, d_copy, e_copy]:
        c.wait_send()
    for k in range(1, 16):
        to, c = rs_copy(k)
        pl.when(to < OWNERS)(c.wait_send)

    @pl.when(me < OWNERS)
    def _():
        for k in range(1, 16):
            to = (me + k) % 16
            copy(
                O.at[d, pl.ds(2 * me, 2)], O.at[d, pl.ds(2 * me, 2)],
                ag_send.at[k], ag_recv.at[me], at_xy(to),
            ).wait_send()


def store(act, gin, gw, gb, act_o, gin_o, gw_o, gb_o, sem):
    copies = [
        pltpu.make_async_copy(src, dst, sem.at[i])
        for i, (src, dst) in enumerate(((gw, gw_o), (act, act_o), (gin, gin_o), (gb, gb_o)))
    ]
    for c in copies:
        c.start()
    for c in copies:
        c.wait()


def per_device(scale, volumes, weight, bias, cotangent):
    vmem = pl.BlockSpec(memory_space=pltpu.VMEM)
    hbm = pl.BlockSpec(memory_space=pltpu.HBM)
    dma = pltpu.SemaphoreType.DMA
    act, gin, gw, gb = pl.pallas_call(
        functools.partial(kernel, scale),
        out_shape=[
            pltpu.VMEM((ROWS, FACE), BF16),
            pltpu.VMEM((ROWS, FACE), BF16),
            pltpu.VMEM((TAPS, ROWS, CHANNELS), F32),
            pltpu.VMEM((1, ROWS), F32),
        ],
        in_specs=[hbm] * 4,
        out_specs=[vmem] * 4,
        scratch_shapes=[
            pltpu.VMEM((2, 3, 8, ROWS, FACE), BF16),
            pltpu.VMEM((2, ROWS, FACE), BF16),
            pltpu.VMEM((2, ROWS, FACE), BF16),
            pltpu.VMEM((2, 3, ROWS, FACE), BF16),
            pltpu.VMEM((2, 3, 9 * ROWS, FACE), BF16),
            pltpu.VMEM((2, UNITS, 16, CHANNELS), F32),
            pltpu.VMEM((2, UNITS, 16, CHANNELS), BF16),
            pltpu.VMEM((UNITS, 16, CHANNELS), BF16),
            pltpu.VMEM((UNITS, 16, CHANNELS), BF16),
            pltpu.VMEM((32, 16, CHANNELS), BF16),
            pltpu.VMEM((2, UNITS, 16, CHANNELS), BF16),
            pltpu.VMEM((2, 8, ROWS, FACE), BF16),
            pltpu.VMEM((7, ROWS, FACE), BF16),
            pltpu.VMEM((TAPS * ROWS, CHANNELS), BF16),
            pltpu.VMEM((CHANNELS, TAPS * ROWS), BF16),
            pltpu.VMEM((1, ROWS), F32),
            dma((4,)), dma((15,)), dma((16,)), dma((32,)), dma((2, 2, 8)), dma((2,)),
            dma((2, 2)), dma((2, 2)),
            dma((2,)), dma((16,)), dma((16,)), dma((16,)), dma((16,)), dma((2,)),
            dma((7,)), dma((7,)),
        ],
        compiler_params=pltpu.CompilerParams(
            collective_id=0, has_side_effects=True, vmem_limit_bytes=48 * 2**20
        ),
    )(
        *(
            pltpu.with_memory_space_constraint(a, pltpu.HBM)
            for a in (
                volumes.reshape(ROWS, FACE),
                weight.reshape(TAPS * ROWS, CHANNELS),
                bias.reshape(1, ROWS),
                cotangent.reshape(ROWS, FACE),
            )
        )
    )
    act, gin, gw, gb = pl.pallas_call(
        store,
        out_shape=[
            jax.ShapeDtypeStruct((ROWS, FACE), BF16),
            jax.ShapeDtypeStruct((ROWS, FACE), BF16),
            jax.ShapeDtypeStruct((TAPS, ROWS, CHANNELS), F32),
            jax.ShapeDtypeStruct((1, ROWS), F32),
        ],
        in_specs=[vmem] * 4,
        out_specs=[hbm] * 4,
        scratch_shapes=[dma((4,))],
    )(*(pltpu.with_memory_space_constraint(a, pltpu.VMEM) for a in (act, gin, gw, gb)))
    shape = (1, ROWS, 1, FACE)
    return act.reshape(shape), gin.reshape(shape), gw, gb.reshape(ROWS)


def solution(mesh):
    scale = 1.0 / math.sqrt(2 * 32 * FACE)
    return jax.shard_map(
        functools.partial(per_device, scale),
        mesh=mesh,
        in_specs=(
            P("dp", "filter", "space", None),
            P(None, "filter", None),
            P("filter"),
            P("dp", "filter", "space", None),
        ),
        out_specs=(
            P("dp", "filter", "space", None),
            P("dp", "filter", "space", None),
            P(None, "filter", None),
            P("filter"),
        ),
        check_vma=False,
    )
```

```python
import functools
import math

import jax
import jax.numpy as jnp
from jax import lax
from jax.experimental import pallas as pl
from jax.experimental.pallas import tpu as pltpu
from jax.sharding import PartitionSpec as P

HEIGHT = 16
BREADTH = 32
FACE = HEIGHT * BREADTH
ROWS = 32
CHANNELS = 256
TAPS = 27
UNITS = 28
OWNERS = UNITS // 2
FAR = sorted(range(1, 16), key=lambda k: -min(k // 4, 4 - k // 4) - min(k % 4, 4 - k % 4))
MESH = pl.DeviceIdType.MESH
F32 = jnp.float32
BF16 = jnp.bfloat16
SHIFTS = [(b, c) for b in (-1, 0, 1) for c in (-1, 0, 1)]


def masks():
    f = lax.broadcasted_iota(jnp.int32, (ROWS, FACE), 1)
    row, col = f // BREADTH, f % BREADTH
    row_ok = {b: (row + b >= 0) & (row + b < HEIGHT) for b in (-1, 1)}
    col_ok = {c: (col + c >= 0) & (col + c < BREADTH) for c in (-1, 1)}
    return row_ok, col_ok


def pull(x, amount, ok):
    return jnp.where(ok, pltpu.roll(x, (-amount) % FACE, 1), 0.0)


def pack(v):
    high = v.astype(BF16).astype(F32)
    low = v - high
    row = lax.broadcasted_iota(jnp.int32, (16, CHANNELS), 0)
    return jnp.where(row == 0, high, jnp.where(row == 1, low, 0.0)).astype(BF16)


def unpack(unit):
    u = unit.astype(F32)
    row = lax.broadcasted_iota(jnp.int32, u.shape, 0)
    return jnp.sum(jnp.where(row < 2, u, 0.0), axis=0, keepdims=True)


def kernel(
    scale,
    vol, w, bias, cot,
    act_o, gin_o, gw_o, gb_o,
    V, COT, CR, ACT, GN, GS, Fp, S, R0, T1, R1, O, N, RG, W, WT, B,
    in_sem, z_send, z_recv, x_send, x_recv, c_sem, g_send, g_recv,
    d_sem, rs_send, rs_recv, ag_send, ag_recv, e_sem, n_send, n_recv,
):
    d = lax.axis_index("dp")
    s = lax.axis_index("space")
    f = lax.axis_index("filter")
    y = s // 8
    zh = (s // 4) % 2
    x = s % 4
    z = zh * 8 + f
    me = y * 4 + x
    sign = 1 - 2 * (z % 2)

    def at_z(k):
        return (d, y * 8 + (k // 8) * 4 + x, k % 8)

    def at_xy(j):
        return (d, (j // 4) * 8 + zh * 4 + j % 4, f)

    def near(k):
        return (z + k + 16) % 16

    other = (1 - d, s, f)

    def copy(src, dst, send, recv, to):
        return pltpu.make_async_remote_copy(
            src_ref=src, dst_ref=dst, send_sem=send, recv_sem=recv,
            device_id=to, device_id_type=MESH,
        )

    barrier = pltpu.get_barrier_semaphore()
    for k in (1, -1, 2, -2, 3, -3, 4, -4):
        pl.semaphore_signal(barrier, inc=1, device_id=at_z(near(k)), device_id_type=MESH)
    for k in range(1, 16):
        pl.semaphore_signal(barrier, inc=1, device_id=at_xy((me + k) % 16), device_id_type=MESH)
    pl.semaphore_signal(barrier, inc=1, device_id=other, device_id_type=MESH)
    loads = [
        pltpu.make_async_copy(src, dst, in_sem.at[i])
        for i, (src, dst) in enumerate(
            ((vol, V.at[zh, 1, f]), (cot, COT.at[zh]), (w, W), (bias, B))
        )
    ]
    for c in loads:
        c.start()
    loads[0].wait()
    loads[1].wait()
    pl.semaphore_wait(barrier, 24)

    def after(p):
        last = x == 3
        x2 = (x + 1) % 4
        y2 = (y + jnp.where(last, p, 0)) % 4
        return y2 * 4 + x2, jnp.where(last, 1 - p, p)

    def before(p):
        first = x == 0
        x2 = (x + 3) % 4
        y2 = (y + 4 - jnp.where(first, 1 - p, 0)) % 4
        return y2 * 4 + x2, jnp.where(first, 1 - p, p)

    sends = []
    x_copies = []

    def place(slot):
        return V.at[slot // 8, 1, slot % 8]

    def shard(o, to):
        slot = near(o)
        c = copy(place(slot), place(slot), z_send.at[len(sends)], z_recv.at[slot], at_z(near(to)))
        c.start()
        sends.append(c)

    def beside(*offsets):
        for o in offsets:
            slot = near(o)
            p, i = slot // 8, slot % 8
            for side, where in ((0, after), (2, before)):
                j, q = where(p)
                c = copy(
                    place(slot), V.at[q, side, i],
                    x_send.at[len(x_copies)], x_recv.at[q, side // 2, i], at_xy(j),
                )
                c.start()
                x_copies.append(c)

    def arrived(*offsets):
        for o in offsets:
            slot = near(o)
            copy(place(slot), place(slot), z_send.at[0], z_recv.at[slot], at_z(near(1))).wait_recv()

    half = near(-4 * sign) // 8
    cot_first = copy(COT.at[zh], CR, c_sem.at[0], c_sem.at[1], at_z(near(4 * sign)))
    cot_copy = copy(CR, COT.at[half], c_sem.at[2], c_sem.at[3], at_z(near(4 * sign)))
    for o in (3, -3, 1, -1):
        shard(0, o)
    beside(0)
    loads[2].wait()
    loads[3].wait()
    WT[...] = W[...].T
    for o in (1, -1):
        arrived(o)
        beside(o)
    for o in (3, -3):
        arrived(o)
        for t in (-o, 1, -1):
            shard(o, t)
    cot_first.start()
    beside(3, -3)
    for o in (2, -2, 4, -4):
        arrived(o)
        beside(o)
    for o in (6, -6):
        arrived(o)
        for t in (1, -1):
            shard(o, t)
    shard(-6 * sign, 2 * sign)
    beside(6, -6)
    cot_first.wait_recv()
    cot_copy.start()
    for o in (5, -5, 7, -7, 8):
        arrived(o)
        beside(o)
    for p in (0, 1):
        for side in (0, 2):
            for i in range(8):
                copy(
                    V.at[p, side, i], V.at[p, side, i],
                    x_send.at[0], x_recv.at[p, side // 2, i], at_xy((me + 1) % 16),
                ).wait_recv()

    first_plane = (y == 0) & (x == 0)
    last_plane = (y == 3) & (x == 3)

    @pl.when(first_plane)
    def _():
        V[0, 0] = jnp.zeros((8, ROWS, FACE), BF16)

    @pl.when(last_plane)
    def _():
        V[1, 2] = jnp.zeros((8, ROWS, FACE), BF16)

    row_ok, col_ok = masks()
    eye = lax.broadcasted_iota(jnp.int32, (ROWS, ROWS), 0) == lax.broadcasted_iota(
        jnp.int32, (ROWS, ROWS), 1
    )
    column = jnp.sum(jnp.where(eye, B[...], 0.0), axis=1, keepdims=True)

    def pre_activation(p):
        taps = jnp.concatenate([W[a * 9 * ROWS : (a + 1) * 9 * ROWS] for a in range(3)], axis=1)
        planes = V[p].reshape(3 * CHANNELS, FACE)
        prod = jnp.dot(taps, planes, preferred_element_type=F32)
        total = column
        for c in (0, -1, 1):
            part = None
            for b in (0, -1, 1):
                i = 3 * (b + 1) + (c + 1)
                term = prod[i * ROWS : (i + 1) * ROWS]
                if b:
                    term = pull(term, BREADTH * b, row_ok[b])
                part = term if part is None else part + term
            if c:
                part = pull(part, c, col_ok[c])
            total = total + part
        return total

    def shifted(p, a, grad):
        for c in (-1, 0, 1):
            moved = pull(grad, -c, col_ok[-c]) if c else grad
            for b in (-1, 0, 1):
                i = 3 * (b + 1) + (c + 1)
                term = pull(moved, -BREADTH * b, row_ok[-b]) if b else moved
                GS[p, a + 1, i * ROWS : (i + 1) * ROWS, :] = term.astype(BF16)

    cot_copy.wait_recv()
    g_copies = []
    bias_total = jnp.zeros((ROWS, 1), F32)
    for p in (0, 1):
        pre = pre_activation(p)
        sig = jax.nn.sigmoid(pre)
        grad = (COT[p].astype(F32) * sig * (1.0 + pre * (1.0 - sig))).astype(BF16)
        GN[p, 1] = grad
        for side, slot, where in ((0, 2, after), (1, 0, before)):
            j, q = where(p)
            c = copy(GN.at[p, 1], GN.at[q, slot], g_send.at[p, side], g_recv.at[q, side], at_xy(j))
            c.start()
            g_copies.append(c)
        ACT[p] = (pre * sig).astype(BF16)
        grad = grad.astype(F32)
        bias_total = bias_total + jnp.sum(grad, axis=1, keepdims=True)
        shifted(p, 0, grad)

    total = None
    for p in (0, 1):
        term = lax.dot_general(
            GS[p, 1], V[p].reshape(3 * CHANNELS, FACE),
            (((1,), (1,)), ((), ())), preferred_element_type=F32,
        )
        total = term if total is None else total + term
    for a in range(3):
        for i in range(9):
            for h in (0, 1):
                piece = total[
                    i * ROWS + h * 16 : i * ROWS + (h + 1) * 16,
                    a * CHANNELS : (a + 1) * CHANNELS,
                ]
                Fp[h, 9 * a + i] = piece
                S[h, 9 * a + i] = piece.astype(BF16)
    eye = lax.broadcasted_iota(jnp.int32, (ROWS, CHANNELS), 0) == lax.broadcasted_iota(
        jnp.int32, (ROWS, CHANNELS), 1
    )
    bias_row = jnp.sum(jnp.where(eye, bias_total, 0.0), axis=0, keepdims=True)
    for h in (0, 1):
        Fp[h, TAPS] = jnp.broadcast_to(bias_row, (16, CHANNELS))
        S[h, TAPS] = pack(bias_row)

    d_copy = copy(S.at[1 - d], R0, d_sem.at[0], d_sem.at[1], other)
    d_copy.start()
    act_o[...] = ACT[zh]
    d_copy.wait_recv()
    summed = Fp[d] + R0[...].astype(F32)
    T1[...] = summed.astype(BF16)
    T1[TAPS] = pack(Fp[d, TAPS, 0:1, :] + unpack(R0[TAPS]))

    def mine(ref, j):
        return ref.at[pl.ds(2 * j, 2)]

    def beyond(k):
        return ((y + k // 4) % 4) * 4 + (x + k) % 4

    def rs_copy(k):
        to = beyond(k)
        return to, copy(mine(T1, to), mine(R1, me), rs_send.at[k], rs_recv.at[me], at_xy(to))

    for k in FAR:
        to, c = rs_copy(k)
        pl.when(to < OWNERS)(c.start)

    for p in (0, 1):
        for side, slot in ((0, 2), (1, 0)):
            copy(
                GN.at[p, 1], GN.at[p, slot], g_send.at[p, side], g_recv.at[p, side], other
            ).wait_recv()
    for p in (0, 1):
        for a in (-1, 1):
            grad = GN[p, a + 1].astype(F32)
            if p == 0 and a == 1:
                grad = jnp.where(first_plane, 0.0, grad)
            if p == 1 and a == -1:
                grad = jnp.where(last_plane, 0.0, grad)
            shifted(p, a, grad)
        part = jnp.dot(
            WT[...], GS[p].reshape(TAPS * ROWS, FACE), preferred_element_type=F32
        )
        for i in range(8):
            N[p, i] = part[i * ROWS : (i + 1) * ROWS].astype(BF16)
    n_copies = []
    for i, o in enumerate((-4 * sign, 3, -3, 2, -2, 1, -1)):
        to = near(o)
        c = copy(N.at[to // 8, to % 8], RG.at[i], n_send.at[i], n_recv.at[i], at_z(to))
        c.start()
        n_copies.append(c)

    @pl.when(me < OWNERS)
    def _():
        R1[pl.ds(2 * me, 2)] = T1[pl.ds(2 * me, 2)]
        for k in range(1, 16):
            source = (me + k) % 16
            copy(
                mine(T1, me), mine(R1, source), rs_send.at[k], rs_recv.at[source], at_xy(source)
            ).wait_recv()
        total = R1[0:2].astype(F32)
        for i in range(1, 16):
            total = total + R1[2 * i : 2 * i + 2].astype(F32)
        O[d, pl.ds(2 * me, 2)] = total.astype(BF16)

        @pl.when(me == OWNERS - 1)
        def _():
            O[d, TAPS] = pack(jnp.sum(total[1, 0:2], axis=0, keepdims=True))

        for k in FAR:
            to = beyond(k)
            copy(
                O.at[d, pl.ds(2 * me, 2)], O.at[d, pl.ds(2 * me, 2)],
                ag_send.at[k], ag_recv.at[me], at_xy(to),
            ).start()

    for k in range(1, 16):
        source = (me + k) % 16

        @pl.when(source < OWNERS)
        def _():
            copy(
                O.at[d, pl.ds(2 * source, 2)], O.at[d, pl.ds(2 * source, 2)],
                ag_send.at[k], ag_recv.at[source], at_xy(source),
            ).wait_recv()

    e_copy = copy(O.at[d], O.at[d], e_sem.at[0], e_sem.at[1], other)
    e_copy.start()

    def finish(h):
        gw_o[:, pl.ds(pl.multiple_of(h * 16, 16), 16), :] = O[h, 0:TAPS].astype(F32) * scale

    finish(d)
    own = N[zh, f].astype(F32)
    for c in n_copies:
        c.wait_recv()
    for i in range(7):
        own = own + RG[i].astype(F32)
    gin_o[...] = own.astype(BF16)
    copy(O.at[1 - d], O.at[1 - d], e_sem.at[0], e_sem.at[1], other).wait_recv()
    finish(1 - d)
    gb_o[...] = unpack(O[0, TAPS])[:, :ROWS] * scale

    for c in sends + x_copies + g_copies + n_copies + [cot_first, cot_copy, d_copy, e_copy]:
        c.wait_send()
    for k in range(1, 16):
        to, c = rs_copy(k)
        pl.when(to < OWNERS)(c.wait_send)

    @pl.when(me < OWNERS)
    def _():
        for k in range(1, 16):
            to = (me + k) % 16
            copy(
                O.at[d, pl.ds(2 * me, 2)], O.at[d, pl.ds(2 * me, 2)],
                ag_send.at[k], ag_recv.at[me], at_xy(to),
            ).wait_send()


def store(act, gin, gw, gb, act_o, gin_o, gw_o, gb_o, sem):
    copies = [
        pltpu.make_async_copy(src, dst, sem.at[i])
        for i, (src, dst) in enumerate(((gw, gw_o), (act, act_o), (gin, gin_o), (gb, gb_o)))
    ]
    for c in copies:
        c.start()
    for c in copies:
        c.wait()


def per_device(scale, volumes, weight, bias, cotangent):
    vmem = pl.BlockSpec(memory_space=pltpu.VMEM)
    hbm = pl.BlockSpec(memory_space=pltpu.HBM)
    dma = pltpu.SemaphoreType.DMA
    act, gin, gw, gb = pl.pallas_call(
        functools.partial(kernel, scale),
        out_shape=[
            pltpu.VMEM((ROWS, FACE), BF16),
            pltpu.VMEM((ROWS, FACE), BF16),
            pltpu.VMEM((TAPS, ROWS, CHANNELS), F32),
            pltpu.VMEM((1, ROWS), F32),
        ],
        in_specs=[hbm] * 4,
        out_specs=[vmem] * 4,
        scratch_shapes=[
            pltpu.VMEM((2, 3, 8, ROWS, FACE), BF16),
            pltpu.VMEM((2, ROWS, FACE), BF16),
            pltpu.VMEM((ROWS, FACE), BF16),
            pltpu.VMEM((2, ROWS, FACE), BF16),
            pltpu.VMEM((2, 3, ROWS, FACE), BF16),
            pltpu.VMEM((2, 3, 9 * ROWS, FACE), BF16),
            pltpu.VMEM((2, UNITS, 16, CHANNELS), F32),
            pltpu.VMEM((2, UNITS, 16, CHANNELS), BF16),
            pltpu.VMEM((UNITS, 16, CHANNELS), BF16),
            pltpu.VMEM((UNITS, 16, CHANNELS), BF16),
            pltpu.VMEM((32, 16, CHANNELS), BF16),
            pltpu.VMEM((2, UNITS, 16, CHANNELS), BF16),
            pltpu.VMEM((2, 8, ROWS, FACE), BF16),
            pltpu.VMEM((7, ROWS, FACE), BF16),
            pltpu.VMEM((TAPS * ROWS, CHANNELS), BF16),
            pltpu.VMEM((CHANNELS, TAPS * ROWS), BF16),
            pltpu.VMEM((1, ROWS), F32),
            dma((4,)), dma((15,)), dma((16,)), dma((32,)), dma((2, 2, 8)), dma((4,)),
            dma((2, 2)), dma((2, 2)),
            dma((2,)), dma((16,)), dma((16,)), dma((16,)), dma((16,)), dma((2,)),
            dma((7,)), dma((7,)),
        ],
        compiler_params=pltpu.CompilerParams(
            collective_id=0, has_side_effects=True, vmem_limit_bytes=48 * 2**20
        ),
    )(
        *(
            pltpu.with_memory_space_constraint(a, pltpu.HBM)
            for a in (
                volumes.reshape(ROWS, FACE),
                weight.reshape(TAPS * ROWS, CHANNELS),
                bias.reshape(1, ROWS),
                cotangent.reshape(ROWS, FACE),
            )
        )
    )
    act, gin, gw, gb = pl.pallas_call(
        store,
        out_shape=[
            jax.ShapeDtypeStruct((ROWS, FACE), BF16),
            jax.ShapeDtypeStruct((ROWS, FACE), BF16),
            jax.ShapeDtypeStruct((TAPS, ROWS, CHANNELS), F32),
            jax.ShapeDtypeStruct((1, ROWS), F32),
        ],
        in_specs=[vmem] * 4,
        out_specs=[hbm] * 4,
        scratch_shapes=[dma((4,))],
    )(*(pltpu.with_memory_space_constraint(a, pltpu.VMEM) for a in (act, gin, gw, gb)))
    shape = (1, ROWS, 1, FACE)
    return act.reshape(shape), gin.reshape(shape), gw, gb.reshape(ROWS)


def solution(mesh):
    scale = 1.0 / math.sqrt(2 * 32 * FACE)
    return jax.shard_map(
        functools.partial(per_device, scale),
        mesh=mesh,
        in_specs=(
            P("dp", "filter", "space", None),
            P(None, "filter", None),
            P("filter"),
            P("dp", "filter", "space", None),
        ),
        out_specs=(
            P("dp", "filter", "space", None),
            P("dp", "filter", "space", None),
            P(None, "filter", None),
            P("filter"),
        ),
        check_vma=False,
    )
```

```python
import functools
import math

import jax
import jax.numpy as jnp
from jax import lax
from jax.experimental import pallas as pl
from jax.experimental.pallas import tpu as pltpu
from jax.sharding import PartitionSpec as P

HEIGHT = 16
BREADTH = 32
FACE = HEIGHT * BREADTH
ROWS = 32
CHANNELS = 256
TAPS = 27
UNITS = 28
OWNERS = UNITS // 2
FAR = sorted(range(1, 16), key=lambda k: -min(k // 4, 4 - k // 4) - min(k % 4, 4 - k % 4))
MESH = pl.DeviceIdType.MESH
F32 = jnp.float32
BF16 = jnp.bfloat16
SHIFTS = [(b, c) for b in (-1, 0, 1) for c in (-1, 0, 1)]


def masks():
    f = lax.broadcasted_iota(jnp.int32, (ROWS, FACE), 1)
    row, col = f // BREADTH, f % BREADTH
    row_ok = {b: (row + b >= 0) & (row + b < HEIGHT) for b in (-1, 1)}
    col_ok = {c: (col + c >= 0) & (col + c < BREADTH) for c in (-1, 1)}
    return row_ok, col_ok


def pull(x, amount, ok):
    return jnp.where(ok, pltpu.roll(x, (-amount) % FACE, 1), 0.0)


def pack(v):
    high = v.astype(BF16).astype(F32)
    low = v - high
    row = lax.broadcasted_iota(jnp.int32, (16, CHANNELS), 0)
    return jnp.where(row == 0, high, jnp.where(row == 1, low, 0.0)).astype(BF16)


def unpack(unit):
    u = unit.astype(F32)
    row = lax.broadcasted_iota(jnp.int32, u.shape, 0)
    return jnp.sum(jnp.where(row < 2, u, 0.0), axis=0, keepdims=True)


def kernel(
    scale,
    vol, w, bias, cot,
    act_o, gin_o, gw_o, gb_o,
    V, COT, CR, ACT, GN, GS, Fp, S, R0, T1, R1, O, N, RG, W, WT, B,
    in_sem, z_send, z_recv, x_send, x_recv, c_sem, g_send, g_recv,
    d_sem, rs_send, rs_recv, ag_send, ag_recv, e_sem, n_send, n_recv,
):
    d = lax.axis_index("dp")
    s = lax.axis_index("space")
    f = lax.axis_index("filter")
    y = s // 8
    zh = (s // 4) % 2
    x = s % 4
    z = zh * 8 + f
    me = y * 4 + x
    sign = 1 - 2 * (z % 2)

    def at_z(k):
        return (d, y * 8 + (k // 8) * 4 + x, k % 8)

    def at_xy(j):
        return (d, (j // 4) * 8 + zh * 4 + j % 4, f)

    def near(k):
        return (z + k + 16) % 16

    other = (1 - d, s, f)

    def copy(src, dst, send, recv, to):
        return pltpu.make_async_remote_copy(
            src_ref=src, dst_ref=dst, send_sem=send, recv_sem=recv,
            device_id=to, device_id_type=MESH,
        )

    barrier = pltpu.get_barrier_semaphore()
    for k in (1, -1, 2, -2, 3, -3, 4, -4):
        pl.semaphore_signal(barrier, inc=1, device_id=at_z(near(k)), device_id_type=MESH)
    for k in range(1, 16):
        pl.semaphore_signal(barrier, inc=1, device_id=at_xy((me + k) % 16), device_id_type=MESH)
    pl.semaphore_signal(barrier, inc=1, device_id=other, device_id_type=MESH)
    loads = [
        pltpu.make_async_copy(src, dst, in_sem.at[i])
        for i, (src, dst) in enumerate(
            ((vol, V.at[zh, 1, f]), (cot, COT.at[zh]), (w, W), (bias, B))
        )
    ]
    for c in loads:
        c.start()
    loads[0].wait()
    loads[1].wait()
    pl.semaphore_wait(barrier, 24)

    def after(p):
        last = x == 3
        x2 = (x + 1) % 4
        y2 = (y + jnp.where(last, p, 0)) % 4
        return y2 * 4 + x2, jnp.where(last, 1 - p, p)

    def before(p):
        first = x == 0
        x2 = (x + 3) % 4
        y2 = (y + 4 - jnp.where(first, 1 - p, 0)) % 4
        return y2 * 4 + x2, jnp.where(first, 1 - p, p)

    sends = []
    x_copies = []

    def place(slot):
        return V.at[slot // 8, 1, slot % 8]

    def shard(o, to):
        slot = near(o)
        c = copy(place(slot), place(slot), z_send.at[len(sends)], z_recv.at[slot], at_z(near(to)))
        c.start()
        sends.append(c)

    def beside(*offsets):
        for o in offsets:
            slot = near(o)
            p, i = slot // 8, slot % 8
            for side, where in ((0, after), (2, before)):
                j, q = where(p)
                c = copy(
                    place(slot), V.at[q, side, i],
                    x_send.at[len(x_copies)], x_recv.at[q, side // 2, i], at_xy(j),
                )
                c.start()
                x_copies.append(c)

    def arrived(*offsets):
        for o in offsets:
            slot = near(o)
            copy(place(slot), place(slot), z_send.at[0], z_recv.at[slot], at_z(near(1))).wait_recv()

    half = near(-4 * sign) // 8
    cot_first = copy(COT.at[zh], CR, c_sem.at[0], c_sem.at[1], at_z(near(4 * sign)))
    cot_copy = copy(CR, COT.at[half], c_sem.at[2], c_sem.at[3], at_z(near(4 * sign)))
    for o in (3, -3, 1, -1):
        shard(0, o)
    beside(0)
    loads[2].wait()
    loads[3].wait()
    WT[...] = W[...].T
    for o in (1, -1):
        arrived(o)
        beside(o)
    for o in (3, -3):
        arrived(o)
        for t in (-o, 1, -1):
            shard(o, t)
    cot_first.start()
    beside(3, -3)
    for o in (2, -2, 4, -4):
        arrived(o)
        beside(o)
    for o in (6, -6):
        arrived(o)
        for t in (1, -1):
            shard(o, t)
    shard(-6 * sign, 2 * sign)
    beside(6, -6)
    cot_first.wait_recv()
    cot_copy.start()
    for o in (5, -5, 7, -7, 8):
        arrived(o)
        beside(o)
    for p in (0, 1):
        for side in (0, 2):
            for i in range(8):
                copy(
                    V.at[p, side, i], V.at[p, side, i],
                    x_send.at[0], x_recv.at[p, side // 2, i], at_xy((me + 1) % 16),
                ).wait_recv()

    first_plane = (y == 0) & (x == 0)
    last_plane = (y == 3) & (x == 3)

    @pl.when(first_plane)
    def _():
        V[0, 0] = jnp.zeros((8, ROWS, FACE), BF16)

    @pl.when(last_plane)
    def _():
        V[1, 2] = jnp.zeros((8, ROWS, FACE), BF16)

    row_ok, col_ok = masks()
    eye = lax.broadcasted_iota(jnp.int32, (ROWS, ROWS), 0) == lax.broadcasted_iota(
        jnp.int32, (ROWS, ROWS), 1
    )
    column = jnp.sum(jnp.where(eye, B[...], 0.0), axis=1, keepdims=True)

    def pre_activation(p):
        taps = jnp.concatenate([W[a * 9 * ROWS : (a + 1) * 9 * ROWS] for a in range(3)], axis=1)
        planes = V[p].reshape(3 * CHANNELS, FACE)
        prod = jnp.dot(taps, planes, preferred_element_type=F32)
        total = column
        for c in (0, -1, 1):
            part = None
            for b in (0, -1, 1):
                i = 3 * (b + 1) + (c + 1)
                term = prod[i * ROWS : (i + 1) * ROWS]
                if b:
                    term = pull(term, BREADTH * b, row_ok[b])
                part = term if part is None else part + term
            if c:
                part = pull(part, c, col_ok[c])
            total = total + part
        return total

    def shifted(p, a, grad):
        for c in (-1, 0, 1):
            moved = pull(grad, -c, col_ok[-c]) if c else grad
            for b in (-1, 0, 1):
                i = 3 * (b + 1) + (c + 1)
                term = pull(moved, -BREADTH * b, row_ok[-b]) if b else moved
                GS[p, a + 1, i * ROWS : (i + 1) * ROWS, :] = term.astype(BF16)

    cot_copy.wait_recv()
    g_copies = []
    bias_total = jnp.zeros((ROWS, 1), F32)
    for p in (0, 1):
        pre = pre_activation(p)
        sig = jax.nn.sigmoid(pre)
        grad = (COT[p].astype(F32) * sig * (1.0 + pre * (1.0 - sig))).astype(BF16)
        GN[p, 1] = grad
        for side, slot, where in ((0, 2, after), (1, 0, before)):
            j, q = where(p)
            c = copy(GN.at[p, 1], GN.at[q, slot], g_send.at[p, side], g_recv.at[q, side], at_xy(j))
            c.start()
            g_copies.append(c)
        ACT[p] = (pre * sig).astype(BF16)
        grad = grad.astype(F32)
        bias_total = bias_total + jnp.sum(grad, axis=1, keepdims=True)
        shifted(p, 0, grad)

    total = None
    for p in (0, 1):
        term = lax.dot_general(
            GS[p, 1], V[p].reshape(3 * CHANNELS, FACE),
            (((1,), (1,)), ((), ())), preferred_element_type=F32,
        )
        total = term if total is None else total + term
    for a in range(3):
        for i in range(9):
            for h in (0, 1):
                piece = total[
                    i * ROWS + h * 16 : i * ROWS + (h + 1) * 16,
                    a * CHANNELS : (a + 1) * CHANNELS,
                ]
                Fp[h, 9 * a + i] = piece
                S[h, 9 * a + i] = piece.astype(BF16)
    eye = lax.broadcasted_iota(jnp.int32, (ROWS, CHANNELS), 0) == lax.broadcasted_iota(
        jnp.int32, (ROWS, CHANNELS), 1
    )
    bias_row = jnp.sum(jnp.where(eye, bias_total, 0.0), axis=0, keepdims=True)
    for h in (0, 1):
        Fp[h, TAPS] = jnp.broadcast_to(bias_row, (16, CHANNELS))
        S[h, TAPS] = pack(bias_row)

    d_copy = copy(S.at[1 - d], R0, d_sem.at[0], d_sem.at[1], other)
    d_copy.start()
    act_o[...] = ACT[zh]
    for p in (0, 1):
        for side, slot in ((0, 2), (1, 0)):
            copy(
                GN.at[p, 1], GN.at[p, slot], g_send.at[p, side], g_recv.at[p, side], other
            ).wait_recv()
    for p in (0, 1):
        for a in (-1, 1):
            grad = GN[p, a + 1].astype(F32)
            if p == 0 and a == 1:
                grad = jnp.where(first_plane, 0.0, grad)
            if p == 1 and a == -1:
                grad = jnp.where(last_plane, 0.0, grad)
            shifted(p, a, grad)
    d_copy.wait_recv()
    summed = Fp[d] + R0[...].astype(F32)
    T1[...] = summed.astype(BF16)
    T1[TAPS] = pack(Fp[d, TAPS, 0:1, :] + unpack(R0[TAPS]))

    def mine(ref, j):
        return ref.at[pl.ds(2 * j, 2)]

    def beyond(k):
        return ((y + k // 4) % 4) * 4 + (x + k) % 4

    def rs_copy(k):
        to = beyond(k)
        return to, copy(mine(T1, to), mine(R1, me), rs_send.at[k], rs_recv.at[me], at_xy(to))

    for k in FAR:
        to, c = rs_copy(k)
        pl.when(to < OWNERS)(c.start)

    for p in (0, 1):
        part = jnp.dot(
            WT[...], GS[p].reshape(TAPS * ROWS, FACE), preferred_element_type=F32
        )
        for i in range(8):
            N[p, i] = part[i * ROWS : (i + 1) * ROWS].astype(BF16)
    n_copies = []
    for i, o in enumerate((-4 * sign, 3, -3, 2, -2, 1, -1)):
        to = near(o)
        c = copy(N.at[to // 8, to % 8], RG.at[i], n_send.at[i], n_recv.at[i], at_z(to))
        c.start()
        n_copies.append(c)

    @pl.when(me < OWNERS)
    def _():
        R1[pl.ds(2 * me, 2)] = T1[pl.ds(2 * me, 2)]
        for k in range(1, 16):
            source = (me + k) % 16
            copy(
                mine(T1, me), mine(R1, source), rs_send.at[k], rs_recv.at[source], at_xy(source)
            ).wait_recv()
        total = R1[0:2].astype(F32)
        for i in range(1, 16):
            total = total + R1[2 * i : 2 * i + 2].astype(F32)
        O[d, pl.ds(2 * me, 2)] = total.astype(BF16)

        @pl.when(me == OWNERS - 1)
        def _():
            O[d, TAPS] = pack(jnp.sum(total[1, 0:2], axis=0, keepdims=True))

        for k in FAR:
            to = beyond(k)
            copy(
                O.at[d, pl.ds(2 * me, 2)], O.at[d, pl.ds(2 * me, 2)],
                ag_send.at[k], ag_recv.at[me], at_xy(to),
            ).start()

    for k in range(1, 16):
        source = (me + k) % 16

        @pl.when(source < OWNERS)
        def _():
            copy(
                O.at[d, pl.ds(2 * source, 2)], O.at[d, pl.ds(2 * source, 2)],
                ag_send.at[k], ag_recv.at[source], at_xy(source),
            ).wait_recv()

    e_copy = copy(O.at[d], O.at[d], e_sem.at[0], e_sem.at[1], other)
    e_copy.start()

    def finish(h):
        gw_o[:, pl.ds(pl.multiple_of(h * 16, 16), 16), :] = O[h, 0:TAPS].astype(F32) * scale

    finish(d)
    own = N[zh, f].astype(F32)
    for c in n_copies:
        c.wait_recv()
    for i in range(7):
        own = own + RG[i].astype(F32)
    gin_o[...] = own.astype(BF16)
    copy(O.at[1 - d], O.at[1 - d], e_sem.at[0], e_sem.at[1], other).wait_recv()
    finish(1 - d)
    gb_o[...] = unpack(O[0, TAPS])[:, :ROWS] * scale

    for c in sends + x_copies + g_copies + n_copies + [cot_first, cot_copy, d_copy, e_copy]:
        c.wait_send()
    for k in range(1, 16):
        to, c = rs_copy(k)
        pl.when(to < OWNERS)(c.wait_send)

    @pl.when(me < OWNERS)
    def _():
        for k in range(1, 16):
            to = (me + k) % 16
            copy(
                O.at[d, pl.ds(2 * me, 2)], O.at[d, pl.ds(2 * me, 2)],
                ag_send.at[k], ag_recv.at[me], at_xy(to),
            ).wait_send()


def store(act, gin, gw, gb, act_o, gin_o, gw_o, gb_o, sem):
    copies = [
        pltpu.make_async_copy(src, dst, sem.at[i])
        for i, (src, dst) in enumerate(((gw, gw_o), (act, act_o), (gin, gin_o), (gb, gb_o)))
    ]
    for c in copies:
        c.start()
    for c in copies:
        c.wait()


def per_device(scale, volumes, weight, bias, cotangent):
    vmem = pl.BlockSpec(memory_space=pltpu.VMEM)
    hbm = pl.BlockSpec(memory_space=pltpu.HBM)
    dma = pltpu.SemaphoreType.DMA
    act, gin, gw, gb = pl.pallas_call(
        functools.partial(kernel, scale),
        out_shape=[
            pltpu.VMEM((ROWS, FACE), BF16),
            pltpu.VMEM((ROWS, FACE), BF16),
            pltpu.VMEM((TAPS, ROWS, CHANNELS), F32),
            pltpu.VMEM((1, ROWS), F32),
        ],
        in_specs=[hbm] * 4,
        out_specs=[vmem] * 4,
        scratch_shapes=[
            pltpu.VMEM((2, 3, 8, ROWS, FACE), BF16),
            pltpu.VMEM((2, ROWS, FACE), BF16),
            pltpu.VMEM((ROWS, FACE), BF16),
            pltpu.VMEM((2, ROWS, FACE), BF16),
            pltpu.VMEM((2, 3, ROWS, FACE), BF16),
            pltpu.VMEM((2, 3, 9 * ROWS, FACE), BF16),
            pltpu.VMEM((2, UNITS, 16, CHANNELS), F32),
            pltpu.VMEM((2, UNITS, 16, CHANNELS), BF16),
            pltpu.VMEM((UNITS, 16, CHANNELS), BF16),
            pltpu.VMEM((UNITS, 16, CHANNELS), BF16),
            pltpu.VMEM((32, 16, CHANNELS), BF16),
            pltpu.VMEM((2, UNITS, 16, CHANNELS), BF16),
            pltpu.VMEM((2, 8, ROWS, FACE), BF16),
            pltpu.VMEM((7, ROWS, FACE), BF16),
            pltpu.VMEM((TAPS * ROWS, CHANNELS), BF16),
            pltpu.VMEM((CHANNELS, TAPS * ROWS), BF16),
            pltpu.VMEM((1, ROWS), F32),
            dma((4,)), dma((15,)), dma((16,)), dma((32,)), dma((2, 2, 8)), dma((4,)),
            dma((2, 2)), dma((2, 2)),
            dma((2,)), dma((16,)), dma((16,)), dma((16,)), dma((16,)), dma((2,)),
            dma((7,)), dma((7,)),
        ],
        compiler_params=pltpu.CompilerParams(
            collective_id=0, has_side_effects=True, vmem_limit_bytes=48 * 2**20
        ),
    )(
        *(
            pltpu.with_memory_space_constraint(a, pltpu.HBM)
            for a in (
                volumes.reshape(ROWS, FACE),
                weight.reshape(TAPS * ROWS, CHANNELS),
                bias.reshape(1, ROWS),
                cotangent.reshape(ROWS, FACE),
            )
        )
    )
    act, gin, gw, gb = pl.pallas_call(
        store,
        out_shape=[
            jax.ShapeDtypeStruct((ROWS, FACE), BF16),
            jax.ShapeDtypeStruct((ROWS, FACE), BF16),
            jax.ShapeDtypeStruct((TAPS, ROWS, CHANNELS), F32),
            jax.ShapeDtypeStruct((1, ROWS), F32),
        ],
        in_specs=[vmem] * 4,
        out_specs=[hbm] * 4,
        scratch_shapes=[dma((4,))],
    )(*(pltpu.with_memory_space_constraint(a, pltpu.VMEM) for a in (act, gin, gw, gb)))
    shape = (1, ROWS, 1, FACE)
    return act.reshape(shape), gin.reshape(shape), gw, gb.reshape(ROWS)


def solution(mesh):
    scale = 1.0 / math.sqrt(2 * 32 * FACE)
    return jax.shard_map(
        functools.partial(per_device, scale),
        mesh=mesh,
        in_specs=(
            P("dp", "filter", "space", None),
            P(None, "filter", None),
            P("filter"),
            P("dp", "filter", "space", None),
        ),
        out_specs=(
            P("dp", "filter", "space", None),
            P("dp", "filter", "space", None),
            P(None, "filter", None),
            P("filter"),
        ),
        check_vma=False,
    )
```
